32 devices in a mesh: row: 8 (over z, core), col: 4 (over y, x).
Axes of the slice: x: 2, y: 2, z: 4, core: 2. Of those that a mesh axis runs over, the one named last changes fastest.
Arguments:
- tensor: float32 [12, 4096, 2048], P(None, 'row', 'col'), may hold values from -6 to 6
- factor_b: float32 [2048, 128], P(('col', 'row')), may hold values from -0.125 to 0.125
- factor_c: float32 [12, 128], replicated, may hold values from -1.75 to 1.75
Outputs:
- a_update: float32 [4096, 128], P(('row', 'col'))
- b_update: float32 [2048, 128], P(('col', 'row'))
The draws below stay inside these ranges and needn't reach their ends.
All inputs are finite; a program needn't handle non-finite values.
Results may differ from the reference program's by a relative error of at most 0.00012.
Values sent between devices are 32-bit elements; how exact they have to be, the bound alone decides.
A program may use at most 64 MiB of HBM per device.

```python
import jax
import jax.numpy as jnp
from jax import lax

K = 12
R = 128
I = 4096
J = 2048


def raised(array, key, source, target, blocks, factor):
    owner, partner = [(jnp.arange(array.shape[dim]) // (array.shape[dim] // blocks)).reshape([-1 if axis == dim else 1 for axis in range(array.ndim)]) for dim in (source, target)]
    chosen = jax.random.permutation(key, blocks)[partner]
    strong = (owner == chosen) | (owner == (partner + blocks // 2) % blocks)
    return jnp.where(strong, factor * array, array)


def level_of(rng, dims, pieces, smallest, high):
    gain, own = 1.0, jax.random.fold_in(rng, 6)
    for position, blocks in pieces:
        steps = jnp.exp(jax.random.uniform(jax.random.fold_in(own, position), (blocks,), jnp.float32, smallest / len(pieces), high / len(pieces)))
        gain = gain * jnp.repeat(steps, dims[position] // blocks).reshape([-1 if axis == position else 1 for axis in range(len(dims))])
    return gain


def noise(rng, extent, spread, reach, shards=(), kind=jnp.bfloat16):
    loudness = level_of(rng, extent, shards, -0.22, 0.18) if shards else 1.0
    entries = jax.random.normal(rng, extent, jnp.float32) * spread * loudness
    return jnp.minimum(jnp.maximum(entries, -reach), reach).astype(kind)


def gaussian_with(own_key, shape, spread, most, split, heavy, held_as=jnp.bfloat16):
    array = spread * jax.random.normal(own_key, shape, jnp.float32)
    if split:
        array = array * level_of(own_key, shape, split, -0.22, 0.18)
    return jnp.clip(raised(array, jax.random.fold_in(own_key, 3), *heavy), -most, most).astype(held_as)


def setup_inputs(seed: int = 0) -> dict:
    seeds = jax.random.split(jax.random.key(seed), 4)
    return {
        "tensor": gaussian_with(seeds[0], (K, I, J), 1.0, 6.0, ((1, 8), (2, 4)), (2, 1, 8, 2.0), jnp.float32),
        "factor_b": noise(seeds[1], (J, R), J ** -0.5, 0.125, ((0, 32),), jnp.float32),
        "factor_c": noise(seeds[2], (K, R), K ** -0.5, 1.75, (), jnp.float32),
    }


EPSILON = 1e-06

def solve_system(rhs, system):
    highest = lax.Precision.HIGHEST
    lower = jnp.linalg.cholesky(system)
    inverse = jax.scipy.linalg.cho_solve((lower, True), jnp.eye(system.shape[0], dtype=system.dtype))
    return jnp.dot(rhs, inverse, precision=highest)

def reference(tensor, factor_b, factor_c):
    highest = lax.Precision.HIGHEST
    c_gram = jnp.dot(factor_c.T, factor_c, precision=highest)
    system_a = c_gram * jnp.dot(factor_b.T, factor_b, precision=highest)

    def mode_one(index, total):
        plane = lax.dynamic_index_in_dim(tensor, index, 0, keepdims=False)
        weights = factor_b * lax.dynamic_index_in_dim(factor_c, index, 0, keepdims=False)
        return total + jnp.dot(plane, weights, precision=highest)
    mttkrp_a = lax.fori_loop(0, K, mode_one, jnp.zeros((I, R), jnp.float32))
    a_update = solve_system(mttkrp_a, system_a)
    column_norm = jnp.sqrt(lax.optimization_barrier(jnp.sum(a_update * a_update, axis=0)) + EPSILON)
    factor_a = a_update / column_norm
    system_b = c_gram * jnp.dot(factor_a.T, factor_a, precision=highest)

    def mode_two(index, total):
        plane = lax.dynamic_index_in_dim(tensor, index, 0, keepdims=False)
        weights = factor_a * lax.dynamic_index_in_dim(factor_c, index, 0, keepdims=False)
        return total + jnp.dot(plane.T, weights, precision=highest)
    mttkrp_b = lax.fori_loop(0, K, mode_two, jnp.zeros((J, R), jnp.float32))
    b_update = solve_system(mttkrp_b, system_b)
    return (a_update, b_update)
```

```python
import functools

import jax
import jax.numpy as jnp
from jax import lax
from jax.experimental import pallas as pl
from jax.experimental.pallas import tpu as pltpu
from jax.sharding import PartitionSpec as P

EPSILON = 1e-06
MESH = pl.DeviceIdType.MESH
HIGHEST = lax.Precision.HIGHEST
PANEL = 8


def exact_dot(left, right):
    return jnp.dot(left, right, precision=HIGHEST, preferred_element_type=jnp.float32)


def fast_dot(left, right):
    return jnp.dot(left, right, preferred_element_type=jnp.float32)


def split(value):
    high = value.astype(jnp.bfloat16)
    low = (value - high.astype(jnp.float32)).astype(jnp.bfloat16)
    return high, low


def negative_inverse(system):
    size = system.shape[0]
    lane = lax.broadcasted_iota(jnp.int32, (PANEL, size), 1)
    sublane = lax.broadcasted_iota(jnp.int32, (PANEL, size), 0)
    whole_lane = lax.broadcasted_iota(jnp.int32, (size, size), 1)
    for base in range(0, size, PANEL):
        rows = system[base : base + PANEL, :]
        inside = (lane >= base) & (lane < base + PANEL)
        solved = jnp.where(inside, jnp.where(lane - base == sublane, -1.0, 0.0), rows)
        columns = jnp.stack(
            [jnp.broadcast_to(rows[:, base + t : base + t + 1], rows.shape) for t in range(PANEL)]
        )
        for t in range(PANEL):
            here = sublane == t
            column = columns[0]
            scale = 1.0 / jnp.broadcast_to(column[t : t + 1, :], rows.shape)
            factor = jnp.where(here, -1.0, column) * scale
            solved = jnp.where(here, 0.0, solved) - factor * solved[t : t + 1, :]
            if t < PANEL - 1:
                rest = columns[1:]
                columns = (
                    jnp.where(here[None], 0.0, rest) - factor[None] * rest[:, t : t + 1, :]
                )
        outside = (whole_lane < base) | (whole_lane >= base + PANEL)
        swept = jnp.where(outside, system, 0.0)
        for t in range(PANEL):
            swept = swept - system[:, base + t : base + t + 1] * solved[t : t + 1, :]
        pieces = [swept[:base], solved, swept[base + PANEL :]]
        system = jnp.concatenate([piece for piece in pieces if piece.shape[0]], axis=0)
    return system


def kernel(
    row_size, col_size,
    tensor, factor_b, factor_c,
    a_out, b_out,
    raw, high, low, piece, c_pad, grams, part_a, recv_a, a_all,
    gram_part, gram_recv, gram_all, acc_b, part_b, recv_b,
    load_sem, piece_send, piece_recv, gramb_send, gramb_recv,
    parta_send, parta_recv, a_send, a_recv,
    gs_send, gs_recv, gg_send, gg_recv, partb_send, partb_recv,
):
    depth, rows, cols = raw.shape
    rank = piece.shape[1]
    own_piece = factor_b.shape[0]
    own_a = rows // col_size
    own_b = cols // row_size
    own_g = rank // row_size
    row = lax.axis_index("row")
    col = lax.axis_index("col")

    def row_peer(d):
        return lax.rem(row + d, row_size)

    def col_peer(d):
        return lax.rem(col + d, col_size)

    def block(index, size):
        return pl.ds(pl.multiple_of(index * size, size), size)

    def loads(k):
        return pltpu.make_async_copy(tensor.at[k], raw.at[k], load_sem.at[k])

    for k in range(depth):
        loads(k).start()

    barrier = pltpu.get_barrier_semaphore()
    for d in range(1, row_size):
        pl.semaphore_signal(barrier, inc=1, device_id=(row_peer(d), col), device_id_type=MESH)
    for d in range(1, col_size):
        pl.semaphore_signal(barrier, inc=1, device_id=(row, col_peer(d)), device_id_type=MESH)
    pl.semaphore_wait(barrier, row_size + col_size - 2)

    def to_row(d, source, target, send, recv):
        return pltpu.make_async_remote_copy(
            src_ref=source, dst_ref=target, send_sem=send.at[d - 1], recv_sem=recv.at[d - 1],
            device_id=(row_peer(d), col), device_id_type=MESH,
        )

    def to_col(d, source, target, send, recv):
        return pltpu.make_async_remote_copy(
            src_ref=source, dst_ref=target, send_sem=send.at[d - 1], recv_sem=recv.at[d - 1],
            device_id=(row, col_peer(d)), device_id_type=MESH,
        )

    def piece_copy(d, owner):
        return to_row(d, factor_b, piece.at[block(owner, own_piece)], piece_send, piece_recv)

    for d in range(1, row_size):
        piece_copy(d, row).start()
    piece[block(row, own_piece), :] = factor_b[...]

    step = 64
    for k in range(depth):
        loads(k).wait()

        def split_rows(index, carry):
            here = block(index, step)
            high[k, here, :], low[k, here, :] = split(raw[k, here, :])
            return carry

        lax.fori_loop(0, rows // step, split_rows, 0)

    c_pad[...] = jnp.zeros(c_pad.shape, jnp.float32)
    c_pad[:depth, :] = factor_c[...]
    c_rows = c_pad[...]
    c_cols = c_rows.T
    c_gram = c_cols[:, 0:1] * c_rows[0:1, :]
    for k in range(1, depth):
        c_gram = c_gram + c_cols[:, k : k + 1] * c_rows[k : k + 1, :]

    for d in range(1, row_size):
        piece_copy(d, row_peer(row_size - d)).wait_recv()

    whole = piece[...]
    grams[col] = exact_dot(whole.T, whole)

    def gramb_copy(d, owner):
        return to_col(d, grams.at[owner], grams.at[owner], gramb_send, gramb_recv)

    for d in range(1, col_size):
        gramb_copy(d, col).start()

    piece_high, piece_low = split(whole)
    both = jnp.concatenate([piece_high, piece_low], axis=1)

    def parta_copy(d, slot):
        return to_col(
            d, part_a.at[block(col_peer(d), own_a)], recv_a.at[slot], parta_send, parta_recv
        )

    group = 4 if depth % 4 == 0 else 1
    for d in list(range(1, col_size)) + [0]:
        owner = col_peer(d)
        here = block(owner, own_a)
        total = jnp.zeros((own_a, rank), jnp.float32)
        for first in range(0, depth, group):
            span = slice(first, first + group)
            flat = (group * own_a, cols)
            left = fast_dot(high[span, here, :].reshape(flat), both)
            right = fast_dot(low[span, here, :].reshape(flat), piece_high)
            summed = left[:, :rank] + (left[:, rank:] + right)
            for k in range(group):
                total = total + summed[k * own_a : (k + 1) * own_a] * c_rows[first + k : first + k + 1, :]
        if d:
            part_a[here, :] = total
            parta_copy(d, d - 1).start()
        else:
            mine = total

    for d in range(1, col_size):
        gramb_copy(d, col_peer(col_size - d)).wait_recv()
    gram_b = grams[0]
    for index in range(1, col_size):
        gram_b = gram_b + grams[index]
    solve_a = negative_inverse(c_gram * gram_b)

    for d in range(1, col_size):
        parta_copy(d, d - 1).wait_recv()
        mine = mine + recv_a[d - 1]
    a_update = -exact_dot(mine, solve_a)
    a_out[...] = a_update
    a_all[block(col, own_a), :] = a_update

    def a_copy(d, owner):
        here = a_all.at[block(owner, own_a)]
        return to_col(d, here, here, a_send, a_recv)

    for d in range(1, col_size):
        a_copy(d, col).start()
    for d in range(1, col_size):
        a_copy(d, col_peer(col_size - d)).wait_recv()

    factor = a_all[...]
    turned = factor.T
    gram_part[...] = exact_dot(turned, factor)

    def gs_copy(d, slot):
        return to_row(
            d, gram_part.at[block(row_peer(d), own_g)], gram_recv.at[slot], gs_send, gs_recv
        )

    for d in range(1, row_size):
        gs_copy(d, d - 1).start()

    turned_high, turned_low = split(turned)
    stacked = jnp.concatenate([turned_high, turned_low], axis=0)

    def mode_two(k):
        left = fast_dot(stacked, high[k])
        right = fast_dot(turned_high, low[k])
        term = (left[:rank] + (left[rank:] + right)) * c_cols[:, k : k + 1]
        if k:
            acc_b[...] += term
        else:
            acc_b[...] = term

    half = depth // 2
    for k in range(half):
        mode_two(k)

    for d in range(1, row_size):
        gs_copy(d, d - 1).wait_recv()
    owned = gram_part[block(row, own_g), :]
    for d in range(1, row_size):
        owned = owned + gram_recv[d - 1]
    gram_all[block(row, own_g), :] = owned

    def gg_copy(d, owner):
        here = gram_all.at[block(owner, own_g)]
        return to_row(d, here, here, gg_send, gg_recv)

    for d in range(1, row_size):
        gg_copy(d, row).start()

    for k in range(half, depth):
        mode_two(k)
    part_b[...] = acc_b[...].T

    def partb_copy(d, slot):
        return to_row(
            d, part_b.at[block(row_peer(d), own_b)], recv_b.at[slot], partb_send, partb_recv
        )

    for d in range(1, row_size):
        partb_copy(d, d - 1).start()

    for d in range(1, row_size):
        gg_copy(d, row_peer(row_size - d)).wait_recv()
    gram_a = gram_all[...]
    diagonal = lax.broadcasted_iota(jnp.int32, (rank, rank), 0) == lax.broadcasted_iota(
        jnp.int32, (rank, rank), 1
    )
    squares = jnp.where(diagonal, gram_a, 0.0)
    inv_row = 1.0 / jnp.sqrt(jnp.sum(squares, axis=0, keepdims=True) + EPSILON)
    inv_col = 1.0 / jnp.sqrt(jnp.sum(squares, axis=1, keepdims=True) + EPSILON)
    solve_b = negative_inverse(c_gram * (gram_a * inv_row * inv_col))

    mine = part_b[block(row, own_b), :]
    for d in range(1, row_size):
        partb_copy(d, d - 1).wait_recv()
        mine = mine + recv_b[d - 1]
    b_out[...] = -exact_dot(mine * inv_row, solve_b)

    for d in range(1, row_size):
        piece_copy(d, row).wait_send()
        gs_copy(d, d - 1).wait_send()
        gg_copy(d, row).wait_send()
        partb_copy(d, d - 1).wait_send()
    for d in range(1, col_size):
        gramb_copy(d, col).wait_send()
        parta_copy(d, d - 1).wait_send()
        a_copy(d, col).wait_send()


def per_device(tensor, factor_b, factor_c):
    depth, rows, cols = tensor.shape
    rank = factor_c.shape[1]
    row_size, col_size = lax.axis_size("row"), lax.axis_size("col")
    own_a, own_b, own_g = rows // col_size, cols // row_size, rank // row_size
    f32, bf16 = jnp.float32, jnp.bfloat16
    vmem = pltpu.VMEM
    row_sem = pltpu.SemaphoreType.DMA((row_size - 1,))
    col_sem = pltpu.SemaphoreType.DMA((col_size - 1,))
    in_vmem = pl.BlockSpec(memory_space=pltpu.VMEM)
    return pl.pallas_call(
        functools.partial(kernel, row_size, col_size),
        out_shape=(
            jax.ShapeDtypeStruct((own_a, rank), f32),
            jax.ShapeDtypeStruct((own_b, rank), f32),
        ),
        in_specs=[pl.BlockSpec(memory_space=pl.ANY), in_vmem, in_vmem],
        out_specs=(in_vmem, in_vmem),
        scratch_shapes=[
            vmem((depth, rows, cols), f32),
            vmem((depth, rows, cols), bf16),
            vmem((depth, rows, cols), bf16),
            vmem((cols, rank), f32),
            vmem((rank, rank), f32),
            vmem((col_size, rank, rank), f32),
            vmem((rows, rank), f32),
            vmem((col_size - 1, own_a, rank), f32),
            vmem((rows, rank), f32),
            vmem((rank, rank), f32),
            vmem((row_size - 1, own_g, rank), f32),
            vmem((rank, rank), f32),
            vmem((rank, cols), f32),
            vmem((cols, rank), f32),
            vmem((row_size - 1, own_b, rank), f32),
            pltpu.SemaphoreType.DMA((depth,)),
            row_sem, row_sem,
            col_sem, col_sem,
            col_sem, col_sem,
            col_sem, col_sem,
            row_sem, row_sem,
            row_sem, row_sem,
            row_sem, row_sem,
        ],
        compiler_params=pltpu.CompilerParams(
            collective_id=0, has_side_effects=True, vmem_limit_bytes=52 * 1024 * 1024
        ),
        cost_estimate=pl.CostEstimate(
            flops=12 * depth * rows * cols * rank,
            bytes_accessed=4 * depth * rows * cols,
            transcendentals=0,
        ),
    )(tensor, factor_b, factor_c)


def solution(mesh):
    placed = (P(None, "row", "col"), P(("col", "row"), None), P())
    return jax.shard_map(
        per_device,
        mesh=mesh,
        in_specs=placed,
        out_specs=(P(("row", "col"), None), P(("col", "row"), None)),
        check_vma=False,
    )
```

```python
import functools

import jax
import jax.numpy as jnp
from jax import lax
from jax.experimental import pallas as pl
from jax.experimental.pallas import tpu as pltpu
from jax.sharding import PartitionSpec as P

EPSILON = 1e-06
MESH = pl.DeviceIdType.MESH
HIGHEST = lax.Precision.HIGHEST
PANEL = 8


def exact_dot(left, right):
    return jnp.dot(left, right, precision=HIGHEST, preferred_element_type=jnp.float32)


def fast_dot(left, right):
    return jnp.dot(left, right, preferred_element_type=jnp.float32)


def split(value):
    high = value.astype(jnp.bfloat16)
    low = (value - high.astype(jnp.float32)).astype(jnp.bfloat16)
    return high, low


def reciprocal(value):
    guess = pl.reciprocal(value, approx=True)
    return guess * (2.0 - value * guess)


def negative_inverse(system):
    size = system.shape[0]
    groups = size // PANEL
    shape = (PANEL, size)
    lane = lax.broadcasted_iota(jnp.int32, shape, 1)
    sublane = lax.broadcasted_iota(jnp.int32, shape, 0)
    whole_lane = lax.broadcasted_iota(jnp.int32, (groups, PANEL, size), 2)
    diagonal = lax.broadcasted_iota(jnp.int32, (size, size), 0) == lax.broadcasted_iota(
        jnp.int32, (size, size), 1
    )
    squares = jnp.where(diagonal, system, 0.0)
    scales = lax.rsqrt(jnp.sum(squares, axis=0, keepdims=True)) * lax.rsqrt(
        jnp.sum(squares, axis=1, keepdims=True)
    )
    system = (system * scales).reshape(groups, PANEL, size)
    for panel in range(groups):
        base = panel * PANEL
        rows = system[panel]
        inside = (lane >= base) & (lane < base + PANEL)
        target = jnp.where(inside, jnp.where(lane - base == sublane, -1.0, 0.0), rows)
        stack = jnp.stack(
            [jnp.broadcast_to(rows[:, base + t : base + t + 1], shape) for t in range(PANEL)]
            + [target]
        )
        grid = jnp.stack(
            [jnp.broadcast_to(stack[:, i : i + 1, :], stack.shape) for i in range(PANEL)]
        )
        for t in range(0, PANEL, 2):
            first, second, rest = grid[:, 0], grid[:, 1], grid[:, 2:]
            one, both, two = first[t], second[t], second[t + 1]
            scale = reciprocal(one * two - both * both)
            upper = (two[None] * rest[t] - both[None] * rest[t + 1]) * scale[None]
            lower = (one[None] * rest[t + 1] - both[None] * rest[t]) * scale[None]
            pieces = []
            for begin, end in ((0, t), (t + 2, PANEL)):
                if begin < end:
                    pieces.append(
                        rest[begin:end]
                        - (
                            first[begin:end, None] * upper[None]
                            + second[begin:end, None] * lower[None]
                        )
                    )
                if begin == 0:
                    pieces += [upper[None], lower[None]]
            grid = jnp.concatenate(pieces, axis=0)
        solved = grid[:, 0]
        outside = (whole_lane < base) | (whole_lane >= base + PANEL)
        swept = jnp.where(outside, system, 0.0)
        terms = [
            system[:, :, base + t : base + t + 1] * solved[t][None] for t in range(PANEL)
        ]
        while len(terms) > 1:
            terms = [terms[i] + terms[i + 1] for i in range(0, len(terms), 2)]
        swept = swept - terms[0]
        own = solved[0]
        for t in range(1, PANEL):
            own = jnp.where(sublane == t, solved[t], own)
        parts = [swept[:panel], own[None], swept[panel + 1 :]]
        system = jnp.concatenate([part for part in parts if part.shape[0]], axis=0)
    return system.reshape(size, size) * scales


def kernel(
    row_size, col_size,
    tensor, factor_b, factor_c,
    a_out, b_out,
    raw, high, low, piece, c_pad, grams, part_a, recv_a, a_all,
    gram_part, gram_recv, gram_all, acc_b, part_b, recv_b,
    load_sem, small_sem, piece_send, piece_recv, pair_send, pair_recv, gramb_send, gramb_recv,
    parta_send, parta_recv, a_send, a_recv,
    gs_send, gs_recv, gg_send, gg_recv, partb_send, partb_recv,
):
    depth, rows, cols = raw.shape
    rank = piece.shape[1]
    own_piece = factor_b.shape[0]
    own_a = rows // col_size
    own_b = cols // row_size
    own_g = rank // row_size
    row = lax.axis_index("row")
    col = lax.axis_index("col")

    def row_peer(d):
        return lax.rem(row + d, row_size)

    def col_peer(d):
        return lax.rem(col + d, col_size)

    def block(index, size):
        return pl.ds(pl.multiple_of(index * size, size), size)

    def loads(k):
        return pltpu.make_async_copy(tensor.at[k], raw.at[k], load_sem.at[k])

    piece_load = pltpu.make_async_copy(
        factor_b, piece.at[block(row, own_piece)], small_sem.at[0]
    )
    c_load = pltpu.make_async_copy(factor_c, c_pad.at[pl.ds(0, depth)], small_sem.at[1])
    c_pad[...] = jnp.zeros(c_pad.shape, jnp.float32)
    piece_load.start()
    c_load.start()
    for k in range(depth):
        loads(k).start()

    barrier = pltpu.get_barrier_semaphore()
    for d in range(1, row_size):
        pl.semaphore_signal(barrier, inc=1, device_id=(row_peer(d), col), device_id_type=MESH)
    for d in range(1, col_size):
        pl.semaphore_signal(barrier, inc=1, device_id=(row, col_peer(d)), device_id_type=MESH)
    pl.semaphore_wait(barrier, row_size + col_size - 2)

    def to_row(d, source, target, send, recv):
        return pltpu.make_async_remote_copy(
            src_ref=source, dst_ref=target, send_sem=send.at[d - 1], recv_sem=recv.at[d - 1],
            device_id=(row_peer(d), col), device_id_type=MESH,
        )

    def to_col(d, source, target, send, recv):
        return pltpu.make_async_remote_copy(
            src_ref=source, dst_ref=target, send_sem=send.at[d - 1], recv_sem=recv.at[d - 1],
            device_id=(row, col_peer(d)), device_id_type=MESH,
        )

    pair = row + 1 - 2 * lax.rem(row, 2)
    chips = row_size // 2

    def chip_peer(d):
        return lax.rem(row + 2 * d, row_size)

    def piece_copy(d, owner):
        here = piece.at[block(owner, own_piece)]
        return pltpu.make_async_remote_copy(
            src_ref=here, dst_ref=here, send_sem=piece_send.at[d], recv_sem=piece_recv.at[d],
            device_id=(chip_peer(d), col), device_id_type=MESH,
        )

    def pair_copy(d, owner):
        here = piece.at[block(owner, own_piece)]
        return pltpu.make_async_remote_copy(
            src_ref=here, dst_ref=here, send_sem=pair_send.at[d], recv_sem=pair_recv.at[d],
            device_id=(pair, col), device_id_type=MESH,
        )

    def partners(d):
        owner = chip_peer(chips - d)
        return owner + 1 - 2 * lax.rem(owner, 2)

    piece_load.wait()
    for d in range(1, chips):
        piece_copy(d, row).start()
    pair_copy(0, row).start()

    step = 64
    for k in range(depth):
        loads(k).wait()

        def split_rows(index, carry):
            here = block(index, step)
            high[k, here, :], low[k, here, :] = split(raw[k, here, :])
            return carry

        lax.fori_loop(0, rows // step, split_rows, 0)

    for d in range(1, chips):
        owner = chip_peer(chips - d)
        piece_copy(d, owner).wait_recv()
        pair_copy(d, owner).start()

    c_load.wait()
    c_rows = c_pad[...]
    c_cols = c_rows.T
    c_gram = c_cols[:, 0:1] * c_rows[0:1, :]
    for k in range(1, depth):
        c_gram = c_gram + c_cols[:, k : k + 1] * c_rows[k : k + 1, :]

    pair_copy(0, pair).wait_recv()
    for d in range(1, chips):
        pair_copy(d, partners(d)).wait_recv()

    whole = piece[...]
    grams[col] = exact_dot(whole.T, whole)

    def gramb_copy(d, owner):
        return to_col(d, grams.at[owner], grams.at[owner], gramb_send, gramb_recv)

    for d in range(1, col_size):
        gramb_copy(d, col).start()

    piece_high, piece_low = split(whole)
    both = jnp.concatenate([piece_high, piece_low], axis=1)

    def parta_copy(d, slot):
        return to_col(
            d, part_a.at[block(col_peer(d), own_a)], recv_a.at[slot], parta_send, parta_recv
        )

    group = 4 if depth % 4 == 0 else 1
    for d in list(range(1, col_size)) + [0]:
        owner = col_peer(d)
        here = block(owner, own_a)
        if d == 0:
            for other in range(1, col_size):
                gramb_copy(other, col_peer(col_size - other)).wait_recv()
            gram_b = grams[0]
            for index in range(1, col_size):
                gram_b = gram_b + grams[index]
        total = jnp.zeros((own_a, rank), jnp.float32)
        for first in range(0, depth, group):
            span = slice(first, first + group)
            flat = (group * own_a, cols)
            left = fast_dot(high[span, here, :].reshape(flat), both)
            right = fast_dot(low[span, here, :].reshape(flat), piece_high)
            summed = left[:, :rank] + (left[:, rank:] + right)
            for k in range(group):
                total = total + summed[k * own_a : (k + 1) * own_a] * c_rows[first + k : first + k + 1, :]
        if d:
            part_a[here, :] = total
            parta_copy(d, d - 1).start()
        else:
            mine = total

    solve_a = negative_inverse(c_gram * gram_b)

    for d in range(1, col_size):
        parta_copy(d, d - 1).wait_recv()
        mine = mine + recv_a[d - 1]
    a_update = -exact_dot(mine, solve_a)
    a_out[...] = a_update
    a_all[block(col, own_a), :] = a_update

    def a_copy(d, owner):
        here = a_all.at[block(owner, own_a)]
        return to_col(d, here, here, a_send, a_recv)

    for d in range(1, col_size):
        a_copy(d, col).start()
    for d in range(1, col_size):
        a_copy(d, col_peer(col_size - d)).wait_recv()

    factor = a_all[...]
    turned = factor.T
    gram_part[...] = exact_dot(turned, factor)

    def gs_copy(d, slot):
        return to_row(
            d, gram_part.at[block(row_peer(d), own_g)], gram_recv.at[slot], gs_send, gs_recv
        )

    for d in range(1, row_size):
        gs_copy(d, d - 1).start()

    turned_high, turned_low = split(turned)
    stacked = jnp.concatenate([turned_high, turned_low], axis=0)

    def mode_two(k):
        left = fast_dot(stacked, high[k])
        right = fast_dot(turned_high, low[k])
        term = (left[:rank] + (left[rank:] + right)) * c_cols[:, k : k + 1]
        if k:
            acc_b[...] += term
        else:
            acc_b[...] = term

    half = depth // 2
    for k in range(half):
        mode_two(k)

    for d in range(1, row_size):
        gs_copy(d, d - 1).wait_recv()
    owned = gram_part[block(row, own_g), :]
    for d in range(1, row_size):
        owned = owned + gram_recv[d - 1]
    gram_all[block(row, own_g), :] = owned

    def gg_copy(d, owner):
        here = gram_all.at[block(owner, own_g)]
        return to_row(d, here, here, gg_send, gg_recv)

    for d in range(1, row_size):
        gg_copy(d, row).start()

    for k in range(half, depth):
        mode_two(k)
    part_b[...] = acc_b[...].T

    def partb_copy(d, slot):
        return to_row(
            d, part_b.at[block(row_peer(d), own_b)], recv_b.at[slot], partb_send, partb_recv
        )

    for d in range(1, row_size):
        partb_copy(d, d - 1).start()

    for d in range(1, row_size):
        gg_copy(d, row_peer(row_size - d)).wait_recv()
    gram_a = gram_all[...]
    diagonal = lax.broadcasted_iota(jnp.int32, (rank, rank), 0) == lax.broadcasted_iota(
        jnp.int32, (rank, rank), 1
    )
    squares = jnp.where(diagonal, gram_a, 0.0)
    inv_row = 1.0 / jnp.sqrt(jnp.sum(squares, axis=0, keepdims=True) + EPSILON)
    inv_col = 1.0 / jnp.sqrt(jnp.sum(squares, axis=1, keepdims=True) + EPSILON)
    solve_b = negative_inverse(c_gram * (gram_a * inv_row * inv_col))

    mine = part_b[block(row, own_b), :]
    for d in range(1, row_size):
        partb_copy(d, d - 1).wait_recv()
        mine = mine + recv_b[d - 1]
    b_out[...] = -exact_dot(mine * inv_row, solve_b)

    pair_copy(0, row).wait_send()
    for d in range(1, chips):
        piece_copy(d, row).wait_send()
        pair_copy(d, chip_peer(chips - d)).wait_send()
    for d in range(1, row_size):
        gs_copy(d, d - 1).wait_send()
        gg_copy(d, row).wait_send()
        partb_copy(d, d - 1).wait_send()
    for d in range(1, col_size):
        gramb_copy(d, col).wait_send()
        parta_copy(d, d - 1).wait_send()
        a_copy(d, col).wait_send()


def per_device(tensor, factor_b, factor_c):
    depth, rows, cols = tensor.shape
    rank = factor_c.shape[1]
    row_size, col_size = lax.axis_size("row"), lax.axis_size("col")
    own_a, own_b, own_g = rows // col_size, cols // row_size, rank // row_size
    f32, bf16 = jnp.float32, jnp.bfloat16
    vmem = pltpu.VMEM
    row_sem = pltpu.SemaphoreType.DMA((row_size - 1,))
    col_sem = pltpu.SemaphoreType.DMA((col_size - 1,))
    chip_sem = pltpu.SemaphoreType.DMA((row_size // 2,))
    in_vmem = pl.BlockSpec(memory_space=pltpu.VMEM)
    return pl.pallas_call(
        functools.partial(kernel, row_size, col_size),
        out_shape=(
            jax.ShapeDtypeStruct((own_a, rank), f32),
            jax.ShapeDtypeStruct((own_b, rank), f32),
        ),
        in_specs=[pl.BlockSpec(memory_space=pl.ANY)] * 3,
        out_specs=(in_vmem, in_vmem),
        scratch_shapes=[
            vmem((depth, rows, cols), f32),
            vmem((depth, rows, cols), bf16),
            vmem((depth, rows, cols), bf16),
            vmem((cols, rank), f32),
            vmem((rank, rank), f32),
            vmem((col_size, rank, rank), f32),
            vmem((rows, rank), f32),
            vmem((col_size - 1, own_a, rank), f32),
            vmem((rows, rank), f32),
            vmem((rank, rank), f32),
            vmem((row_size - 1, own_g, rank), f32),
            vmem((rank, rank), f32),
            vmem((rank, cols), f32),
            vmem((cols, rank), f32),
            vmem((row_size - 1, own_b, rank), f32),
            pltpu.SemaphoreType.DMA((depth,)),
            pltpu.SemaphoreType.DMA((2,)),
            chip_sem, chip_sem, chip_sem, chip_sem,
            col_sem, col_sem,
            col_sem, col_sem,
            col_sem, col_sem,
            row_sem, row_sem,
            row_sem, row_sem,
            row_sem, row_sem,
        ],
        compiler_params=pltpu.CompilerParams(
            collective_id=0, has_side_effects=True, vmem_limit_bytes=60 * 1024 * 1024
        ),
        cost_estimate=pl.CostEstimate(
            flops=12 * depth * rows * cols * rank,
            bytes_accessed=4 * depth * rows * cols,
            transcendentals=0,
        ),
    )(tensor, factor_b, factor_c)


def solution(mesh):
    placed = (P(None, "row", "col"), P(("col", "row"), None), P())
    return jax.shard_map(
        per_device,
        mesh=mesh,
        in_specs=placed,
        out_specs=(P(("row", "col"), None), P(("col", "row"), None)),
        check_vma=False,
    )
```

```python
import functools

import jax
import jax.numpy as jnp
from jax import lax
from jax.experimental import pallas as pl
from jax.experimental.pallas import tpu as pltpu
from jax.sharding import PartitionSpec as P

EPSILON = 1e-06
MESH = pl.DeviceIdType.MESH
HIGHEST = lax.Precision.HIGHEST
PANEL = 8


def exact_dot(left, right):
    return jnp.dot(left, right, precision=HIGHEST, preferred_element_type=jnp.float32)


def fast_dot(left, right):
    return jnp.dot(left, right, preferred_element_type=jnp.float32)


def split(value):
    high = value.astype(jnp.bfloat16)
    low = (value - high.astype(jnp.float32)).astype(jnp.bfloat16)
    return high, low


def reciprocal(value):
    guess = pl.reciprocal(value, approx=True)
    return guess * (2.0 - value * guess)


def thirds(value):
    high = value.astype(jnp.bfloat16).astype(jnp.float32)
    rest = value - high
    middle = rest.astype(jnp.bfloat16).astype(jnp.float32)
    return high, middle, rest - middle


def outer_product(left, right):
    l0, l1, l2 = thirds(left)
    r0, r1, r2 = thirds(right)
    lefts = jnp.concatenate([l0, l0, l1, l0, l1, l2], axis=0).astype(jnp.bfloat16)
    rights = jnp.concatenate([r0, r1, r0, r2, r1, r0], axis=0).astype(jnp.bfloat16)
    return lax.dot_general(
        lefts, rights, (((0,), (0,)), ((), ())), preferred_element_type=jnp.float32
    )


def negative_inverse(system):
    size = system.shape[0]
    groups = size // PANEL
    shape = (PANEL, size)
    lane = lax.broadcasted_iota(jnp.int32, shape, 1)
    sublane = lax.broadcasted_iota(jnp.int32, shape, 0)
    whole_lane = lax.broadcasted_iota(jnp.int32, (groups, PANEL, size), 2)
    diagonal = lax.broadcasted_iota(jnp.int32, (size, size), 0) == lax.broadcasted_iota(
        jnp.int32, (size, size), 1
    )
    squares = jnp.where(diagonal, system, 0.0)
    scales = lax.rsqrt(jnp.sum(squares, axis=0, keepdims=True)) * lax.rsqrt(
        jnp.sum(squares, axis=1, keepdims=True)
    )
    system = (system * scales).reshape(groups, PANEL, size)
    for panel in range(groups):
        base = panel * PANEL
        rows = system[panel]
        inside = (lane >= base) & (lane < base + PANEL)
        target = jnp.where(inside, jnp.where(lane - base == sublane, -1.0, 0.0), rows)
        stack = jnp.stack(
            [jnp.broadcast_to(rows[:, base + t : base + t + 1], shape) for t in range(PANEL)]
            + [target]
        )
        grid = jnp.stack(
            [jnp.broadcast_to(stack[:, i : i + 1, :], stack.shape) for i in range(PANEL)]
        )
        for t in range(0, PANEL, 2):
            first, second, rest = grid[:, 0], grid[:, 1], grid[:, 2:]
            one, both, two = first[t], second[t], second[t + 1]
            scale = reciprocal(one * two - both * both)
            upper = (two[None] * rest[t] - both[None] * rest[t + 1]) * scale[None]
            lower = (one[None] * rest[t + 1] - both[None] * rest[t]) * scale[None]
            pieces = []
            for begin, end in ((0, t), (t + 2, PANEL)):
                if begin < end:
                    pieces.append(
                        rest[begin:end]
                        - (
                            first[begin:end, None] * upper[None]
                            + second[begin:end, None] * lower[None]
                        )
                    )
                if begin == 0:
                    pieces += [upper[None], lower[None]]
            grid = jnp.concatenate(pieces, axis=0)
        solved = grid[:, 0]
        own = solved[0]
        for t in range(1, PANEL):
            own = jnp.where(sublane == t, solved[t], own)
        if panel + 1 < groups:
            after = system[panel + 1]
            terms = [
                jnp.broadcast_to(after[:, base + t : base + t + 1], shape) * solved[t]
                for t in range(PANEL)
            ]
            while len(terms) > 1:
                terms = [terms[i] + terms[i + 1] for i in range(0, len(terms), 2)]
            ahead = jnp.where(inside, 0.0, after) - terms[0]
        outside = (whole_lane < base) | (whole_lane >= base + PANEL)
        product = outer_product(rows, own).reshape(groups, PANEL, size)
        swept = jnp.where(outside, system, 0.0) - product
        parts = [swept[:panel], own[None]]
        if panel + 1 < groups:
            parts += [ahead[None], swept[panel + 2 :]]
        system = jnp.concatenate([part for part in parts if part.shape[0]], axis=0)
    return system.reshape(size, size) * scales


def kernel(
    row_size, col_size,
    tensor, factor_b, factor_c,
    a_out, b_out,
    raw, high, low, piece, c_pad, grams, part_a, recv_a, a_all,
    gram_part, gram_recv, gram_all, acc_b, part_b, recv_b,
    load_sem, small_sem, piece_send, piece_recv, pair_send, pair_recv, gramb_send, gramb_recv,
    parta_send, parta_recv, a_send, a_recv,
    gs_send, gs_recv, gg_send, gg_recv, partb_send, partb_recv,
):
    depth, rows, cols = raw.shape
    rank = piece.shape[1]
    own_piece = factor_b.shape[0]
    own_a = rows // col_size
    own_b = cols // row_size
    own_g = rank // row_size
    row = lax.axis_index("row")
    col = lax.axis_index("col")

    def row_peer(d):
        return lax.rem(row + d, row_size)

    def col_peer(d):
        return lax.rem(col + d, col_size)

    def block(index, size):
        return pl.ds(pl.multiple_of(index * size, size), size)

    def loads(k):
        return pltpu.make_async_copy(tensor.at[k], raw.at[k], load_sem.at[k])

    piece_load = pltpu.make_async_copy(
        factor_b, piece.at[block(row, own_piece)], small_sem.at[0]
    )
    c_load = pltpu.make_async_copy(factor_c, c_pad.at[pl.ds(0, depth)], small_sem.at[1])
    c_pad[...] = jnp.zeros(c_pad.shape, jnp.float32)
    piece_load.start()
    c_load.start()
    for k in range(depth):
        loads(k).start()

    barrier = pltpu.get_barrier_semaphore()
    for d in range(1, row_size):
        pl.semaphore_signal(barrier, inc=1, device_id=(row_peer(d), col), device_id_type=MESH)
    for d in range(1, col_size):
        pl.semaphore_signal(barrier, inc=1, device_id=(row, col_peer(d)), device_id_type=MESH)
    pl.semaphore_wait(barrier, row_size + col_size - 2)

    def to_row(d, source, target, send, recv):
        return pltpu.make_async_remote_copy(
            src_ref=source, dst_ref=target, send_sem=send.at[d - 1], recv_sem=recv.at[d - 1],
            device_id=(row_peer(d), col), device_id_type=MESH,
        )

    def to_col(d, source, target, send, recv):
        return pltpu.make_async_remote_copy(
            src_ref=source, dst_ref=target, send_sem=send.at[d - 1], recv_sem=recv.at[d - 1],
            device_id=(row, col_peer(d)), device_id_type=MESH,
        )

    pair = row + 1 - 2 * lax.rem(row, 2)
    chips = row_size // 2

    def chip_peer(d):
        return lax.rem(row + 2 * d, row_size)

    def piece_copy(d, owner):
        here = piece.at[block(owner, own_piece)]
        return pltpu.make_async_remote_copy(
            src_ref=here, dst_ref=here, send_sem=piece_send.at[d], recv_sem=piece_recv.at[d],
            device_id=(chip_peer(d), col), device_id_type=MESH,
        )

    def pair_copy(d, owner):
        here = piece.at[block(owner, own_piece)]
        return pltpu.make_async_remote_copy(
            src_ref=here, dst_ref=here, send_sem=pair_send.at[d], recv_sem=pair_recv.at[d],
            device_id=(pair, col), device_id_type=MESH,
        )

    def partners(d):
        owner = chip_peer(chips - d)
        return owner + 1 - 2 * lax.rem(owner, 2)

    piece_load.wait()
    for d in range(1, chips):
        piece_copy(d, row).start()
    pair_copy(0, row).start()

    step = 64
    for k in range(depth):
        loads(k).wait()

        def split_rows(index, carry):
            here = block(index, step)
            high[k, here, :], low[k, here, :] = split(raw[k, here, :])
            return carry

        lax.fori_loop(0, rows // step, split_rows, 0)

    for d in range(1, chips):
        owner = chip_peer(chips - d)
        piece_copy(d, owner).wait_recv()
        pair_copy(d, owner).start()

    c_load.wait()
    c_rows = c_pad[...]
    c_cols = c_rows.T
    c_gram = c_cols[:, 0:1] * c_rows[0:1, :]
    for k in range(1, depth):
        c_gram = c_gram + c_cols[:, k : k + 1] * c_rows[k : k + 1, :]

    pair_copy(0, pair).wait_recv()
    for d in range(1, chips):
        pair_copy(d, partners(d)).wait_recv()

    whole = piece[...]
    grams[col] = exact_dot(whole.T, whole)

    def gramb_copy(d, owner):
        return to_col(d, grams.at[owner], grams.at[owner], gramb_send, gramb_recv)

    for d in range(1, col_size):
        gramb_copy(d, col).start()

    piece_high, piece_low = split(whole)
    both = jnp.concatenate([piece_high, piece_low], axis=1)

    def parta_copy(d, slot):
        return to_col(
            d, part_a.at[block(col_peer(d), own_a)], recv_a.at[slot], parta_send, parta_recv
        )

    group = 4 if depth % 4 == 0 else 1
    for d in list(range(1, col_size)) + [0]:
        owner = col_peer(d)
        here = block(owner, own_a)
        if d == 0:
            for other in range(1, col_size):
                gramb_copy(other, col_peer(col_size - other)).wait_recv()
            gram_b = grams[0]
            for index in range(1, col_size):
                gram_b = gram_b + grams[index]
        total = jnp.zeros((own_a, rank), jnp.float32)
        for first in range(0, depth, group):
            span = slice(first, first + group)
            flat = (group * own_a, cols)
            left = fast_dot(high[span, here, :].reshape(flat), both)
            right = fast_dot(low[span, here, :].reshape(flat), piece_high)
            summed = left[:, :rank] + (left[:, rank:] + right)
            for k in range(group):
                total = total + summed[k * own_a : (k + 1) * own_a] * c_rows[first + k : first + k + 1, :]
        if d:
            part_a[here, :] = total
            parta_copy(d, d - 1).start()
        else:
            mine = total

    solve_a = negative_inverse(c_gram * gram_b)

    for d in range(1, col_size):
        parta_copy(d, d - 1).wait_recv()
        mine = mine + recv_a[d - 1]
    a_update = -exact_dot(mine, solve_a)
    a_out[...] = a_update
    a_all[block(col, own_a), :] = a_update

    def a_copy(d, owner):
        here = a_all.at[block(owner, own_a)]
        return to_col(d, here, here, a_send, a_recv)

    for d in range(1, col_size):
        a_copy(d, col).start()
    for d in range(1, col_size):
        a_copy(d, col_peer(col_size - d)).wait_recv()

    factor = a_all[...]
    turned = factor.T
    gram_part[...] = exact_dot(turned, factor)

    def gs_copy(d, slot):
        return to_row(
            d, gram_part.at[block(row_peer(d), own_g)], gram_recv.at[slot], gs_send, gs_recv
        )

    for d in range(1, row_size):
        gs_copy(d, d - 1).start()

    turned_high, turned_low = split(turned)
    stacked = jnp.concatenate([turned_high, turned_low], axis=0)

    def mode_two(k):
        left = fast_dot(stacked, high[k])
        right = fast_dot(turned_high, low[k])
        term = (left[:rank] + (left[rank:] + right)) * c_cols[:, k : k + 1]
        if k:
            acc_b[...] += term
        else:
            acc_b[...] = term

    half = depth // 2
    for k in range(half):
        mode_two(k)

    for d in range(1, row_size):
        gs_copy(d, d - 1).wait_recv()
    owned = gram_part[block(row, own_g), :]
    for d in range(1, row_size):
        owned = owned + gram_recv[d - 1]
    gram_all[block(row, own_g), :] = owned

    def gg_copy(d, owner):
        here = gram_all.at[block(owner, own_g)]
        return to_row(d, here, here, gg_send, gg_recv)

    for d in range(1, row_size):
        gg_copy(d, row).start()

    for k in range(half, depth):
        mode_two(k)
    part_b[...] = acc_b[...].T

    def partb_copy(d, slot):
        return to_row(
            d, part_b.at[block(row_peer(d), own_b)], recv_b.at[slot], partb_send, partb_recv
        )

    for d in range(1, row_size):
        partb_copy(d, d - 1).start()

    for d in range(1, row_size):
        gg_copy(d, row_peer(row_size - d)).wait_recv()
    gram_a = gram_all[...]
    diagonal = lax.broadcasted_iota(jnp.int32, (rank, rank), 0) == lax.broadcasted_iota(
        jnp.int32, (rank, rank), 1
    )
    squares = jnp.where(diagonal, gram_a, 0.0)
    inv_row = 1.0 / jnp.sqrt(jnp.sum(squares, axis=0, keepdims=True) + EPSILON)
    inv_col = 1.0 / jnp.sqrt(jnp.sum(squares, axis=1, keepdims=True) + EPSILON)
    solve_b = negative_inverse(c_gram * (gram_a * inv_row * inv_col))

    mine = part_b[block(row, own_b), :]
    for d in range(1, row_size):
        partb_copy(d, d - 1).wait_recv()
        mine = mine + recv_b[d - 1]
    b_out[...] = -exact_dot(mine * inv_row, solve_b)

    pair_copy(0, row).wait_send()
    for d in range(1, chips):
        piece_copy(d, row).wait_send()
        pair_copy(d, chip_peer(chips - d)).wait_send()
    for d in range(1, row_size):
        gs_copy(d, d - 1).wait_send()
        gg_copy(d, row).wait_send()
        partb_copy(d, d - 1).wait_send()
    for d in range(1, col_size):
        gramb_copy(d, col).wait_send()
        parta_copy(d, d - 1).wait_send()
        a_copy(d, col).wait_send()


def finish(a_update, b_update, a_out, b_out, sems):
    copies = [
        pltpu.make_async_copy(a_update, a_out, sems.at[0]),
        pltpu.make_async_copy(b_update, b_out, sems.at[1]),
    ]
    for copy in copies:
        copy.start()
    for copy in copies:
        copy.wait()


def per_device(tensor, factor_b, factor_c):
    depth, rows, cols = tensor.shape
    rank = factor_c.shape[1]
    row_size, col_size = lax.axis_size("row"), lax.axis_size("col")
    own_a, own_b, own_g = rows // col_size, cols // row_size, rank // row_size
    f32, bf16 = jnp.float32, jnp.bfloat16
    vmem = pltpu.VMEM
    row_sem = pltpu.SemaphoreType.DMA((row_size - 1,))
    col_sem = pltpu.SemaphoreType.DMA((col_size - 1,))
    chip_sem = pltpu.SemaphoreType.DMA((row_size // 2,))
    in_vmem = pl.BlockSpec(memory_space=pltpu.VMEM)
    shapes = (
        jax.ShapeDtypeStruct((own_a, rank), f32),
        jax.ShapeDtypeStruct((own_b, rank), f32),
    )
    updates = pl.pallas_call(
        functools.partial(kernel, row_size, col_size),
        out_shape=shapes,
        in_specs=[pl.BlockSpec(memory_space=pltpu.HBM)] * 3,
        out_specs=(in_vmem, in_vmem),
        scratch_shapes=[
            vmem((depth, rows, cols), f32),
            vmem((depth, rows, cols), bf16),
            vmem((depth, rows, cols), bf16),
            vmem((cols, rank), f32),
            vmem((rank, rank), f32),
            vmem((col_size, rank, rank), f32),
            vmem((rows, rank), f32),
            vmem((col_size - 1, own_a, rank), f32),
            vmem((rows, rank), f32),
            vmem((rank, rank), f32),
            vmem((row_size - 1, own_g, rank), f32),
            vmem((rank, rank), f32),
            vmem((rank, cols), f32),
            vmem((cols, rank), f32),
            vmem((row_size - 1, own_b, rank), f32),
            pltpu.SemaphoreType.DMA((depth,)),
            pltpu.SemaphoreType.DMA((2,)),
            chip_sem, chip_sem, chip_sem, chip_sem,
            col_sem, col_sem,
            col_sem, col_sem,
            col_sem, col_sem,
            row_sem, row_sem,
            row_sem, row_sem,
            row_sem, row_sem,
        ],
        compiler_params=pltpu.CompilerParams(
            collective_id=0, has_side_effects=True, vmem_limit_bytes=52 * 1024 * 1024
        ),
        cost_estimate=pl.CostEstimate(
            flops=12 * depth * rows * cols * rank,
            bytes_accessed=4 * depth * rows * cols,
            transcendentals=0,
        ),
    )(tensor, factor_b, factor_c)
    anywhere = pl.BlockSpec(memory_space=pl.ANY)
    return pl.pallas_call(
        finish,
        out_shape=shapes,
        in_specs=[anywhere] * 2,
        out_specs=(anywhere, anywhere),
        scratch_shapes=[pltpu.SemaphoreType.DMA((2,))],
        compiler_params=pltpu.CompilerParams(vmem_limit_bytes=1024 * 1024),
    )(*updates)


def solution(mesh):
    placed = (P(None, "row", "col"), P(("col", "row"), None), P())
    return jax.shard_map(
        per_device,
        mesh=mesh,
        in_specs=placed,
        out_specs=(P(("row", "col"), None), P(("col", "row"), None)),
        check_vma=False,
    )
```

```python
import functools

import jax
import jax.numpy as jnp
from jax import lax
from jax.experimental import pallas as pl
from jax.experimental.pallas import tpu as pltpu
from jax.sharding import PartitionSpec as P

EPSILON = 1e-06
MESH = pl.DeviceIdType.MESH
HIGHEST = lax.Precision.HIGHEST
PANEL = 8


def exact_dot(left, right):
    return jnp.dot(left, right, precision=HIGHEST, preferred_element_type=jnp.float32)


def fast_dot(left, right):
    return jnp.dot(left, right, preferred_element_type=jnp.float32)


def split(value):
    high = value.astype(jnp.bfloat16)
    low = (value - high.astype(jnp.float32)).astype(jnp.bfloat16)
    return high, low


def reciprocal(value):
    guess = pl.reciprocal(value, approx=True)
    return guess * (2.0 - value * guess)


def thirds(value):
    high = value.astype(jnp.bfloat16).astype(jnp.float32)
    rest = value - high
    middle = rest.astype(jnp.bfloat16).astype(jnp.float32)
    return high, middle, rest - middle


def outer_product(left, right):
    l0, l1, l2 = thirds(left)
    r0, r1, r2 = thirds(right)
    lefts = jnp.concatenate([l0, l0, l1, l0, l1, l2], axis=0).astype(jnp.bfloat16)
    rights = jnp.concatenate([r0, r1, r0, r2, r1, r0], axis=0).astype(jnp.bfloat16)
    return lax.dot_general(
        lefts, rights, (((0,), (0,)), ((), ())), preferred_element_type=jnp.float32
    )


def negative_inverse(system, beside=None):
    size = system.shape[0]
    groups = size // PANEL
    shape = (PANEL, size)
    lane = lax.broadcasted_iota(jnp.int32, shape, 1)
    sublane = lax.broadcasted_iota(jnp.int32, shape, 0)
    whole_lane = lax.broadcasted_iota(jnp.int32, (groups, PANEL, size), 2)
    diagonal = lax.broadcasted_iota(jnp.int32, (size, size), 0) == lax.broadcasted_iota(
        jnp.int32, (size, size), 1
    )
    squares = jnp.where(diagonal, system, 0.0)
    scales = lax.rsqrt(jnp.sum(squares, axis=0, keepdims=True)) * lax.rsqrt(
        jnp.sum(squares, axis=1, keepdims=True)
    )
    system = (system * scales).reshape(groups, PANEL, size)
    for panel in range(groups):
        base = panel * PANEL
        rows = system[panel]
        inside = (lane >= base) & (lane < base + PANEL)
        target = jnp.where(inside, jnp.where(lane - base == sublane, -1.0, 0.0), rows)
        stack = jnp.stack(
            [jnp.broadcast_to(rows[:, base + t : base + t + 1], shape) for t in range(PANEL)]
            + [target]
        )
        grid = jnp.stack(
            [jnp.broadcast_to(stack[:, i : i + 1, :], stack.shape) for i in range(PANEL)]
        )
        for t in range(0, PANEL, 2):
            first, second, rest = grid[:, 0], grid[:, 1], grid[:, 2:]
            one, both, two = first[t], second[t], second[t + 1]
            scale = reciprocal(one * two - both * both)
            upper = (two[None] * rest[t] - both[None] * rest[t + 1]) * scale[None]
            lower = (one[None] * rest[t + 1] - both[None] * rest[t]) * scale[None]
            pieces = []
            for begin, end in ((0, t), (t + 2, PANEL)):
                if begin < end:
                    pieces.append(
                        rest[begin:end]
                        - (
                            first[begin:end, None] * upper[None]
                            + second[begin:end, None] * lower[None]
                        )
                    )
                if begin == 0:
                    pieces += [upper[None], lower[None]]
            grid = jnp.concatenate(pieces, axis=0)
        solved = grid[:, 0]
        own = solved[0]
        for t in range(1, PANEL):
            own = jnp.where(sublane == t, solved[t], own)
        if panel + 1 < groups:
            after = system[panel + 1]
            terms = [
                jnp.broadcast_to(after[:, base + t : base + t + 1], shape) * solved[t]
                for t in range(PANEL)
            ]
            while len(terms) > 1:
                terms = [terms[i] + terms[i + 1] for i in range(0, len(terms), 2)]
            ahead = jnp.where(inside, 0.0, after) - terms[0]
        outside = (whole_lane < base) | (whole_lane >= base + PANEL)
        product = outer_product(rows, own).reshape(groups, PANEL, size)
        swept = jnp.where(outside, system, 0.0) - product
        parts = [swept[:panel], own[None]]
        if panel + 1 < groups:
            parts += [ahead[None], swept[panel + 2 :]]
        system = jnp.concatenate([part for part in parts if part.shape[0]], axis=0)
        if beside is not None:
            beside(panel)
    return system.reshape(size, size) * scales


def kernel(
    row_size, col_size,
    tensor, factor_b, factor_c,
    a_out, b_out,
    raw, high, low, piece, c_pad, grams, part_a, recv_a, a_all,
    gram_part, gram_recv, gram_all, acc_b, part_b, recv_b,
    load_sem, small_sem, piece_send, piece_recv, pair_send, pair_recv, gramb_send, gramb_recv,
    parta_send, parta_recv, a_send, a_recv,
    gs_send, gs_recv, gg_send, gg_recv, partb_send, partb_recv,
):
    depth, rows, cols = raw.shape
    rank = piece.shape[1]
    own_piece = factor_b.shape[0]
    own_a = rows // col_size
    own_b = cols // row_size
    own_g = rank // row_size
    row = lax.axis_index("row")
    col = lax.axis_index("col")

    def row_peer(d):
        return lax.rem(row + d, row_size)

    def col_peer(d):
        return lax.rem(col + d, col_size)

    def block(index, size):
        return pl.ds(pl.multiple_of(index * size, size), size)

    def loads(k):
        return pltpu.make_async_copy(tensor.at[k], raw.at[k], load_sem.at[k])

    piece_load = pltpu.make_async_copy(
        factor_b, piece.at[block(row, own_piece)], small_sem.at[0]
    )
    c_load = pltpu.make_async_copy(factor_c, c_pad.at[pl.ds(0, depth)], small_sem.at[1])
    c_pad[...] = jnp.zeros(c_pad.shape, jnp.float32)
    piece_load.start()
    c_load.start()
    for k in range(depth):
        loads(k).start()

    barrier = pltpu.get_barrier_semaphore()
    for d in range(1, row_size):
        pl.semaphore_signal(barrier, inc=1, device_id=(row_peer(d), col), device_id_type=MESH)
    for d in range(1, col_size):
        pl.semaphore_signal(barrier, inc=1, device_id=(row, col_peer(d)), device_id_type=MESH)
    pl.semaphore_wait(barrier, row_size + col_size - 2)

    def to_row(d, source, target, send, recv):
        return pltpu.make_async_remote_copy(
            src_ref=source, dst_ref=target, send_sem=send.at[d - 1], recv_sem=recv.at[d - 1],
            device_id=(row_peer(d), col), device_id_type=MESH,
        )

    def to_col(d, source, target, send, recv):
        return pltpu.make_async_remote_copy(
            src_ref=source, dst_ref=target, send_sem=send.at[d - 1], recv_sem=recv.at[d - 1],
            device_id=(row, col_peer(d)), device_id_type=MESH,
        )

    pair = row + 1 - 2 * lax.rem(row, 2)
    chips = row_size // 2

    def chip_peer(d):
        return lax.rem(row + 2 * d, row_size)

    def piece_copy(d, owner):
        here = piece.at[block(owner, own_piece)]
        return pltpu.make_async_remote_copy(
            src_ref=here, dst_ref=here, send_sem=piece_send.at[d], recv_sem=piece_recv.at[d],
            device_id=(chip_peer(d), col), device_id_type=MESH,
        )

    def pair_copy(d, owner):
        here = piece.at[block(owner, own_piece)]
        return pltpu.make_async_remote_copy(
            src_ref=here, dst_ref=here, send_sem=pair_send.at[d], recv_sem=pair_recv.at[d],
            device_id=(pair, col), device_id_type=MESH,
        )

    def partners(d):
        owner = chip_peer(chips - d)
        return owner + 1 - 2 * lax.rem(owner, 2)

    piece_load.wait()
    for d in range(1, chips):
        piece_copy(d, row).start()
    pair_copy(0, row).start()

    step = 64
    for k in range(depth):
        loads(k).wait()

        def split_rows(index, carry):
            here = block(index, step)
            high[k, here, :], low[k, here, :] = split(raw[k, here, :])
            return carry

        lax.fori_loop(0, rows // step, split_rows, 0)

    for d in range(1, chips):
        owner = chip_peer(chips - d)
        piece_copy(d, owner).wait_recv()
        pair_copy(d, owner).start()

    c_load.wait()
    c_rows = c_pad[...]
    c_cols = c_rows.T
    c_gram = c_cols[:, 0:1] * c_rows[0:1, :]
    for k in range(1, depth):
        c_gram = c_gram + c_cols[:, k : k + 1] * c_rows[k : k + 1, :]

    pair_copy(0, pair).wait_recv()
    for d in range(1, chips):
        pair_copy(d, partners(d)).wait_recv()

    whole = piece[...]
    grams[col] = exact_dot(whole.T, whole)

    def gramb_copy(d, owner):
        return to_col(d, grams.at[owner], grams.at[owner], gramb_send, gramb_recv)

    for d in range(1, col_size):
        gramb_copy(d, col).start()

    piece_high, piece_low = split(whole)
    both = jnp.concatenate([piece_high, piece_low], axis=1)

    def parta_copy(d, slot):
        return to_col(
            d, part_a.at[block(col_peer(d), own_a)], recv_a.at[slot], parta_send, parta_recv
        )

    group = 4 if depth % 4 == 0 else 1
    state = {}

    def mode_one(d, first):
        owner = col_peer(d)
        here = block(owner, own_a)
        span = slice(first, first + group)
        flat = (group * own_a, cols)
        left = fast_dot(high[span, here, :].reshape(flat), both)
        right = fast_dot(low[span, here, :].reshape(flat), piece_high)
        summed = left[:, :rank] + (left[:, rank:] + right)
        total = state["total"] if first else 0.0
        for k in range(group):
            total = total + summed[k * own_a : (k + 1) * own_a] * c_rows[first + k : first + k + 1, :]
        state["total"] = total
        if first + group == depth and d:
            part_a[here, :] = total
            parta_copy(d, d - 1).start()

    order = list(range(1, col_size)) + [0]
    items = [(d, first) for d in order for first in range(0, depth, group)]
    lead = len(items) * 5 // 12
    for item in items[:lead]:
        mode_one(*item)
    items = items[lead:]
    panels = rank // PANEL
    share = -(-len(items) // (panels // 2))

    def beside_a(panel):
        for item in items[panel * share : (panel + 1) * share]:
            mode_one(*item)

    for d in range(1, col_size):
        gramb_copy(d, col_peer(col_size - d)).wait_recv()
    gram_b = grams[0]
    for index in range(1, col_size):
        gram_b = gram_b + grams[index]
    solve_a = negative_inverse(c_gram * gram_b, beside_a)

    mine = state["total"]
    for d in range(1, col_size):
        parta_copy(d, d - 1).wait_recv()
        mine = mine + recv_a[d - 1]
    a_update = -exact_dot(mine, solve_a)
    a_out[...] = a_update
    a_all[block(col, own_a), :] = a_update

    def a_copy(d, owner):
        here = a_all.at[block(owner, own_a)]
        return to_col(d, here, here, a_send, a_recv)

    for d in range(1, col_size):
        a_copy(d, col).start()
    for d in range(1, col_size):
        a_copy(d, col_peer(col_size - d)).wait_recv()

    factor = a_all[...]
    turned = factor.T
    gram_part[...] = exact_dot(turned, factor)

    def gs_copy(d, slot):
        return to_row(
            d, gram_part.at[block(row_peer(d), own_g)], gram_recv.at[slot], gs_send, gs_recv
        )

    for d in range(1, row_size):
        gs_copy(d, d - 1).start()

    turned_high, turned_low = split(turned)
    stacked = jnp.concatenate([turned_high, turned_low], axis=0)

    width = cols // 2

    def mode_two(k, half):
        lanes = slice(half * width, (half + 1) * width)
        left = fast_dot(stacked, high[k, :, lanes])
        right = fast_dot(turned_high, low[k, :, lanes])
        term = (left[:rank] + (left[rank:] + right)) * c_cols[:, k : k + 1]
        if k:
            acc_b[half] += term
        else:
            acc_b[half] = term

    def partb_copy(owner, slot):
        d = lax.rem(owner - row + row_size, row_size)
        return pltpu.make_async_remote_copy(
            src_ref=part_b.at[block(owner, own_b)], dst_ref=recv_b.at[slot],
            send_sem=partb_send.at[d - 1], recv_sem=partb_recv.at[d - 1],
            device_id=(owner, col), device_id_type=MESH,
        )

    def send_half(half):
        part_b[half * width : (half + 1) * width, :] = acc_b[half].T
        for owner in range(half * row_size // 2, (half + 1) * row_size // 2):

            @pl.when(row != owner)
            def _():
                partb_copy(owner, lax.rem(owner - row + row_size, row_size) - 1).start()

    early = 2 * depth // 3
    for k in range(early):
        mode_two(k, 0)

    for d in range(1, row_size):
        gs_copy(d, d - 1).wait_recv()
    owned = gram_part[block(row, own_g), :]
    for d in range(1, row_size):
        owned = owned + gram_recv[d - 1]
    gram_all[block(row, own_g), :] = owned

    def gg_copy(d, owner):
        here = gram_all.at[block(owner, own_g)]
        return to_row(d, here, here, gg_send, gg_recv)

    for d in range(1, row_size):
        gg_copy(d, row).start()

    for k in range(early, depth):
        mode_two(k, 0)
    send_half(0)
    for k in range(depth // 2):
        mode_two(k, 1)

    def beside_b(panel):
        k = depth // 2 + panel
        if k < depth:
            mode_two(k, 1)
            if k == depth - 1:
                send_half(1)

    for d in range(1, row_size):
        gg_copy(d, row_peer(row_size - d)).wait_recv()
    gram_a = gram_all[...]
    diagonal = lax.broadcasted_iota(jnp.int32, (rank, rank), 0) == lax.broadcasted_iota(
        jnp.int32, (rank, rank), 1
    )
    squares = jnp.where(diagonal, gram_a, 0.0)
    inv_row = 1.0 / jnp.sqrt(jnp.sum(squares, axis=0, keepdims=True) + EPSILON)
    inv_col = 1.0 / jnp.sqrt(jnp.sum(squares, axis=1, keepdims=True) + EPSILON)
    solve_b = negative_inverse(c_gram * (gram_a * inv_row * inv_col), beside_b)

    mine = part_b[block(row, own_b), :]
    for d in range(1, row_size):
        partb_copy(row_peer(d), d - 1).wait_recv()
        mine = mine + recv_b[d - 1]
    b_out[...] = -exact_dot(mine * inv_row, solve_b)

    pair_copy(0, row).wait_send()
    for d in range(1, chips):
        piece_copy(d, row).wait_send()
        pair_copy(d, chip_peer(chips - d)).wait_send()
    for d in range(1, row_size):
        gs_copy(d, d - 1).wait_send()
        gg_copy(d, row).wait_send()
        partb_copy(row_peer(d), d - 1).wait_send()
    for d in range(1, col_size):
        gramb_copy(d, col).wait_send()
        parta_copy(d, d - 1).wait_send()
        a_copy(d, col).wait_send()


def finish(a_update, b_update, a_out, b_out, sems):
    copies = [
        pltpu.make_async_copy(a_update, a_out, sems.at[0]),
        pltpu.make_async_copy(b_update, b_out, sems.at[1]),
    ]
    for copy in copies:
        copy.start()
    for copy in copies:
        copy.wait()


def per_device(tensor, factor_b, factor_c):
    depth, rows, cols = tensor.shape
    rank = factor_c.shape[1]
    row_size, col_size = lax.axis_size("row"), lax.axis_size("col")
    own_a, own_b, own_g = rows // col_size, cols // row_size, rank // row_size
    f32, bf16 = jnp.float32, jnp.bfloat16
    vmem = pltpu.VMEM
    row_sem = pltpu.SemaphoreType.DMA((row_size - 1,))
    col_sem = pltpu.SemaphoreType.DMA((col_size - 1,))
    chip_sem = pltpu.SemaphoreType.DMA((row_size // 2,))
    in_vmem = pl.BlockSpec(memory_space=pltpu.VMEM)
    shapes = (
        jax.ShapeDtypeStruct((own_a, rank), f32),
        jax.ShapeDtypeStruct((own_b, rank), f32),
    )
    updates = pl.pallas_call(
        functools.partial(kernel, row_size, col_size),
        out_shape=shapes,
        in_specs=[pl.BlockSpec(memory_space=pltpu.HBM)] * 3,
        out_specs=(in_vmem, in_vmem),
        scratch_shapes=[
            vmem((depth, rows, cols), f32),
            vmem((depth, rows, cols), bf16),
            vmem((depth, rows, cols), bf16),
            vmem((cols, rank), f32),
            vmem((rank, rank), f32),
            vmem((col_size, rank, rank), f32),
            vmem((rows, rank), f32),
            vmem((col_size - 1, own_a, rank), f32),
            vmem((rows, rank), f32),
            vmem((rank, rank), f32),
            vmem((row_size - 1, own_g, rank), f32),
            vmem((rank, rank), f32),
            vmem((2, rank, cols // 2), f32),
            vmem((cols, rank), f32),
            vmem((row_size - 1, own_b, rank), f32),
            pltpu.SemaphoreType.DMA((depth,)),
            pltpu.SemaphoreType.DMA((2,)),
            chip_sem, chip_sem, chip_sem, chip_sem,
            col_sem, col_sem,
            col_sem, col_sem,
            col_sem, col_sem,
            row_sem, row_sem,
            row_sem, row_sem,
            row_sem, row_sem,
        ],
        compiler_params=pltpu.CompilerParams(
            collective_id=0, has_side_effects=True, vmem_limit_bytes=52 * 1024 * 1024
        ),
        cost_estimate=pl.CostEstimate(
            flops=12 * depth * rows * cols * rank,
            bytes_accessed=4 * depth * rows * cols,
            transcendentals=0,
        ),
    )(tensor, factor_b, factor_c)
    anywhere = pl.BlockSpec(memory_space=pl.ANY)
    return pl.pallas_call(
        finish,
        out_shape=shapes,
        in_specs=[anywhere] * 2,
        out_specs=(anywhere, anywhere),
        scratch_shapes=[pltpu.SemaphoreType.DMA((2,))],
        compiler_params=pltpu.CompilerParams(vmem_limit_bytes=1024 * 1024),
    )(*updates)


def solution(mesh):
    placed = (P(None, "row", "col"), P(("col", "row"), None), P())
    return jax.shard_map(
        per_device,
        mesh=mesh,
        in_specs=placed,
        out_specs=(P(("row", "col"), None), P(("col", "row"), None)),
        check_vma=False,
    )
```

```python
import functools

import jax
import jax.numpy as jnp
from jax import lax
from jax.experimental import pallas as pl
from jax.experimental.pallas import tpu as pltpu
from jax.sharding import PartitionSpec as P

EPSILON = 1e-06
MESH = pl.DeviceIdType.MESH
HIGHEST = lax.Precision.HIGHEST
PANEL = 8


def exact_dot(left, right):
    return jnp.dot(left, right, precision=HIGHEST, preferred_element_type=jnp.float32)


def fast_dot(left, right):
    return jnp.dot(left, right, preferred_element_type=jnp.float32)


def split(value):
    high = value.astype(jnp.bfloat16)
    low = (value - high.astype(jnp.float32)).astype(jnp.bfloat16)
    return high, low


def reciprocal(value):
    guess = pl.reciprocal(value, approx=True)
    return guess * (2.0 - value * guess)


def thirds(value):
    high = value.astype(jnp.bfloat16).astype(jnp.float32)
    rest = value - high
    middle = rest.astype(jnp.bfloat16).astype(jnp.float32)
    return high, middle, rest - middle


def outer_product(left, right):
    l0, l1, l2 = thirds(left)
    r0, r1, r2 = thirds(right)
    lefts = jnp.concatenate([l0, l0, l1, l0, l1, l2], axis=0).astype(jnp.bfloat16)
    rights = jnp.concatenate([r0, r1, r0, r2, r1, r0], axis=0).astype(jnp.bfloat16)
    return lax.dot_general(
        lefts, rights, (((0,), (0,)), ((), ())), preferred_element_type=jnp.float32
    )


def negative_inverse(system):
    size = system.shape[0]
    groups = size // PANEL
    shape = (PANEL, size)
    lane = lax.broadcasted_iota(jnp.int32, shape, 1)
    sublane = lax.broadcasted_iota(jnp.int32, shape, 0)
    whole_lane = lax.broadcasted_iota(jnp.int32, (groups, PANEL, size), 2)
    diagonal = lax.broadcasted_iota(jnp.int32, (size, size), 0) == lax.broadcasted_iota(
        jnp.int32, (size, size), 1
    )
    squares = jnp.where(diagonal, system, 0.0)
    scales = lax.rsqrt(jnp.sum(squares, axis=0, keepdims=True)) * lax.rsqrt(
        jnp.sum(squares, axis=1, keepdims=True)
    )
    system = (system * scales).reshape(groups, PANEL, size)
    for panel in range(groups):
        base = panel * PANEL
        rows = system[panel]
        inside = (lane >= base) & (lane < base + PANEL)
        target = jnp.where(inside, jnp.where(lane - base == sublane, -1.0, 0.0), rows)
        stack = jnp.stack(
            [jnp.broadcast_to(rows[:, base + t : base + t + 1], shape) for t in range(PANEL)]
            + [target]
        )
        for t in range(0, PANEL, 2):
            first, second, rest = stack[0], stack[1], stack[2:]
            one = jnp.broadcast_to(first[t : t + 1, :], shape)
            both = jnp.broadcast_to(second[t : t + 1, :], shape)
            two = jnp.broadcast_to(second[t + 1 : t + 2, :], shape)
            upper, lower = sublane == t, sublane == t + 1
            scale = reciprocal(one * two - both * both)
            left = jnp.where(upper, -two, jnp.where(lower, both, first * two - second * both))
            right = jnp.where(upper, both, jnp.where(lower, -one, second * one - first * both))
            left, right = left * scale, right * scale
            kept = jnp.where((upper | lower)[None], 0.0, rest)
            stack = kept - (
                left[None] * rest[:, t : t + 1, :] + right[None] * rest[:, t + 1 : t + 2, :]
            )
        own = stack[0]
        if panel + 1 < groups:
            after = system[panel + 1]
            terms = [
                jnp.broadcast_to(after[:, base + t : base + t + 1], shape) * own[t : t + 1, :]
                for t in range(PANEL)
            ]
            while len(terms) > 1:
                terms = [terms[i] + terms[i + 1] for i in range(0, len(terms), 2)]
            ahead = jnp.where(inside, 0.0, after) - terms[0]
        outside = (whole_lane < base) | (whole_lane >= base + PANEL)
        product = outer_product(rows, own).reshape(groups, PANEL, size)
        swept = jnp.where(outside, system, 0.0) - product
        parts = [swept[:panel], own[None]]
        if panel + 1 < groups:
            parts += [ahead[None], swept[panel + 2 :]]
        system = jnp.concatenate([part for part in parts if part.shape[0]], axis=0)
    return system.reshape(size, size) * scales


def kernel(
    row_size, col_size,
    tensor, factor_b, factor_c,
    a_out, b_out,
    raw, parts, piece, c_pad, grams, part_a, recv_a, a_all,
    gram_part, gram_recv, gram_all, acc_b, part_b, recv_b,
    load_sem, small_sem, piece_send, piece_recv, pair_send, pair_recv, gramb_send, gramb_recv,
    parta_send, parta_recv, a_send, a_recv,
    gs_send, gs_recv, gg_send, gg_recv, partb_send, partb_recv,
):
    depth, rows, cols = raw.shape
    rank = piece.shape[1]
    own_piece = factor_b.shape[0]
    own_a = rows // col_size
    own_b = cols // row_size
    own_g = rank // row_size
    row = lax.axis_index("row")
    col = lax.axis_index("col")

    def row_peer(d):
        return lax.rem(row + d, row_size)

    def col_peer(d):
        return lax.rem(col + d, col_size)

    def block(index, size):
        return pl.ds(pl.multiple_of(index * size, size), size)

    def loads(k):
        return pltpu.make_async_copy(tensor.at[k], raw.at[k], load_sem.at[k])

    piece_load = pltpu.make_async_copy(
        factor_b, piece.at[block(row, own_piece)], small_sem.at[0]
    )
    c_load = pltpu.make_async_copy(factor_c, c_pad.at[pl.ds(0, depth)], small_sem.at[1])
    c_pad[...] = jnp.zeros(c_pad.shape, jnp.float32)
    piece_load.start()
    c_load.start()
    for k in range(depth):
        loads(k).start()

    barrier = pltpu.get_barrier_semaphore()
    for d in range(1, row_size):
        pl.semaphore_signal(barrier, inc=1, device_id=(row_peer(d), col), device_id_type=MESH)
    for d in range(1, col_size):
        pl.semaphore_signal(barrier, inc=1, device_id=(row, col_peer(d)), device_id_type=MESH)
    pl.semaphore_wait(barrier, row_size + col_size - 2)

    def to_row(d, source, target, send, recv):
        return pltpu.make_async_remote_copy(
            src_ref=source, dst_ref=target, send_sem=send.at[d - 1], recv_sem=recv.at[d - 1],
            device_id=(row_peer(d), col), device_id_type=MESH,
        )

    def to_col(d, source, target, send, recv):
        return pltpu.make_async_remote_copy(
            src_ref=source, dst_ref=target, send_sem=send.at[d - 1], recv_sem=recv.at[d - 1],
            device_id=(row, col_peer(d)), device_id_type=MESH,
        )

    pair = row + 1 - 2 * lax.rem(row, 2)
    chips = row_size // 2

    def chip_peer(d):
        return lax.rem(row + 2 * d, row_size)

    def piece_copy(d, owner):
        here = piece.at[block(owner, own_piece)]
        return pltpu.make_async_remote_copy(
            src_ref=here, dst_ref=here, send_sem=piece_send.at[d], recv_sem=piece_recv.at[d],
            device_id=(chip_peer(d), col), device_id_type=MESH,
        )

    def pair_copy(d, owner):
        here = piece.at[block(owner, own_piece)]
        return pltpu.make_async_remote_copy(
            src_ref=here, dst_ref=here, send_sem=pair_send.at[d], recv_sem=pair_recv.at[d],
            device_id=(pair, col), device_id_type=MESH,
        )

    def partners(d):
        owner = chip_peer(chips - d)
        return owner + 1 - 2 * lax.rem(owner, 2)

    piece_load.wait()
    for d in range(1, chips):
        piece_copy(d, row).start()
    pair_copy(0, row).start()

    step = 64
    for k in range(depth):
        loads(k).wait()

        def split_rows(index, carry):
            here = block(index, step)
            parts[k, here, :cols], parts[k, here, cols:] = split(raw[k, here, :])
            return carry

        lax.fori_loop(0, rows // step, split_rows, 0)

    for d in range(1, chips):
        owner = chip_peer(chips - d)
        piece_copy(d, owner).wait_recv()
        pair_copy(d, owner).start()

    c_load.wait()
    c_rows = c_pad[...]
    c_cols = c_rows.T
    c_gram = c_cols[:, 0:1] * c_rows[0:1, :]
    for k in range(1, depth):
        c_gram = c_gram + c_cols[:, k : k + 1] * c_rows[k : k + 1, :]

    pair_copy(0, pair).wait_recv()
    for d in range(1, chips):
        pair_copy(d, partners(d)).wait_recv()

    whole = piece[...]
    grams[col] = exact_dot(whole.T, whole)

    def gramb_copy(d, owner):
        return to_col(d, grams.at[owner], grams.at[owner], gramb_send, gramb_recv)

    for d in range(1, col_size):
        gramb_copy(d, col).start()

    piece_high, piece_low = split(whole)
    both = jnp.concatenate(
        [
            jnp.concatenate([piece_high, piece_low], axis=1),
            jnp.concatenate([piece_high, jnp.zeros_like(piece_low)], axis=1),
        ],
        axis=0,
    )

    def parta_copy(d, slot):
        return to_col(
            d, part_a.at[block(col_peer(d), own_a)], recv_a.at[slot], parta_send, parta_recv
        )

    group = 4 if depth % 4 == 0 else 1
    for d in list(range(1, col_size)) + [0]:
        owner = col_peer(d)
        here = block(owner, own_a)
        if d == 0:
            for other in range(1, col_size):
                gramb_copy(other, col_peer(col_size - other)).wait_recv()
            gram_b = grams[0]
            for index in range(1, col_size):
                gram_b = gram_b + grams[index]
        total = jnp.zeros((own_a, rank), jnp.float32)
        for first in range(0, depth, group):
            span = slice(first, first + group)
            product = fast_dot(parts[span, here, :].reshape(group * own_a, 2 * cols), both)
            summed = product[:, :rank] + product[:, rank:]
            for k in range(group):
                total = total + summed[k * own_a : (k + 1) * own_a] * c_rows[first + k : first + k + 1, :]
        if d:
            part_a[here, :] = total
            parta_copy(d, d - 1).start()
        else:
            mine = total

    solve_a = negative_inverse(c_gram * gram_b)

    for d in range(1, col_size):
        parta_copy(d, d - 1).wait_recv()
        mine = mine + recv_a[d - 1]
    a_update = -exact_dot(mine, solve_a)
    a_out[...] = a_update
    a_all[block(col, own_a), :] = a_update

    def a_copy(d, owner):
        here = a_all.at[block(owner, own_a)]
        return to_col(d, here, here, a_send, a_recv)

    for d in range(1, col_size):
        a_copy(d, col).start()
    for d in range(1, col_size):
        a_copy(d, col_peer(col_size - d)).wait_recv()

    factor = a_all[...]
    turned = factor.T
    gram_part[...] = exact_dot(turned, factor)

    def gs_copy(d, slot):
        return to_row(
            d, gram_part.at[block(row_peer(d), own_g)], gram_recv.at[slot], gs_send, gs_recv
        )

    for d in range(1, row_size):
        gs_copy(d, d - 1).start()

    turned_high, turned_low = split(turned)
    stacked = jnp.concatenate([turned_high, turned_low], axis=0)

    def mode_two(k):
        left = fast_dot(stacked, parts[k, :, :cols])
        right = fast_dot(turned_high, parts[k, :, cols:])
        term = (left[:rank] + (left[rank:] + right)) * c_cols[:, k : k + 1]
        if k:
            acc_b[...] += term
        else:
            acc_b[...] = term

    half = depth // 2
    for k in range(half):
        mode_two(k)

    for d in range(1, row_size):
        gs_copy(d, d - 1).wait_recv()
    owned = gram_part[block(row, own_g), :]
    for d in range(1, row_size):
        owned = owned + gram_recv[d - 1]
    gram_all[block(row, own_g), :] = owned

    def gg_copy(d, owner):
        here = gram_all.at[block(owner, own_g)]
        return to_row(d, here, here, gg_send, gg_recv)

    for d in range(1, row_size):
        gg_copy(d, row).start()

    for k in range(half, depth):
        mode_two(k)
    part_b[...] = acc_b[...].T

    def partb_copy(d, slot):
        return to_row(
            d, part_b.at[block(row_peer(d), own_b)], recv_b.at[slot], partb_send, partb_recv
        )

    for d in range(1, row_size):
        partb_copy(d, d - 1).start()

    for d in range(1, row_size):
        gg_copy(d, row_peer(row_size - d)).wait_recv()
    gram_a = gram_all[...]
    diagonal = lax.broadcasted_iota(jnp.int32, (rank, rank), 0) == lax.broadcasted_iota(
        jnp.int32, (rank, rank), 1
    )
    squares = jnp.where(diagonal, gram_a, 0.0)
    inv_row = 1.0 / jnp.sqrt(jnp.sum(squares, axis=0, keepdims=True) + EPSILON)
    inv_col = 1.0 / jnp.sqrt(jnp.sum(squares, axis=1, keepdims=True) + EPSILON)
    solve_b = negative_inverse(c_gram * (gram_a * inv_row * inv_col))

    mine = part_b[block(row, own_b), :]
    for d in range(1, row_size):
        partb_copy(d, d - 1).wait_recv()
        mine = mine + recv_b[d - 1]
    b_out[...] = -exact_dot(mine * inv_row, solve_b)

    pair_copy(0, row).wait_send()
    for d in range(1, chips):
        piece_copy(d, row).wait_send()
        pair_copy(d, chip_peer(chips - d)).wait_send()
    for d in range(1, row_size):
        gs_copy(d, d - 1).wait_send()
        gg_copy(d, row).wait_send()
        partb_copy(d, d - 1).wait_send()
    for d in range(1, col_size):
        gramb_copy(d, col).wait_send()
        parta_copy(d, d - 1).wait_send()
        a_copy(d, col).wait_send()


def finish(a_update, b_update, a_out, b_out, sems):
    copies = [
        pltpu.make_async_copy(a_update, a_out, sems.at[0]),
        pltpu.make_async_copy(b_update, b_out, sems.at[1]),
    ]
    for copy in copies:
        copy.start()
    for copy in copies:
        copy.wait()


def per_device(tensor, factor_b, factor_c):
    depth, rows, cols = tensor.shape
    rank = factor_c.shape[1]
    row_size, col_size = lax.axis_size("row"), lax.axis_size("col")
    own_a, own_b, own_g = rows // col_size, cols // row_size, rank // row_size
    f32, bf16 = jnp.float32, jnp.bfloat16
    vmem = pltpu.VMEM
    row_sem = pltpu.SemaphoreType.DMA((row_size - 1,))
    col_sem = pltpu.SemaphoreType.DMA((col_size - 1,))
    chip_sem = pltpu.SemaphoreType.DMA((row_size // 2,))
    in_vmem = pl.BlockSpec(memory_space=pltpu.VMEM)
    shapes = (
        jax.ShapeDtypeStruct((own_a, rank), f32),
        jax.ShapeDtypeStruct((own_b, rank), f32),
    )
    updates = pl.pallas_call(
        functools.partial(kernel, row_size, col_size),
        out_shape=shapes,
        in_specs=[pl.BlockSpec(memory_space=pltpu.HBM)] * 3,
        out_specs=(in_vmem, in_vmem),
        scratch_shapes=[
            vmem((depth, rows, cols), f32),
            vmem((depth, rows, 2 * cols), bf16),
            vmem((cols, rank), f32),
            vmem((rank, rank), f32),
            vmem((col_size, rank, rank), f32),
            vmem((rows, rank), f32),
            vmem((col_size - 1, own_a, rank), f32),
            vmem((rows, rank), f32),
            vmem((rank, rank), f32),
            vmem((row_size - 1, own_g, rank), f32),
            vmem((rank, rank), f32),
            vmem((rank, cols), f32),
            vmem((cols, rank), f32),
            vmem((row_size - 1, own_b, rank), f32),
            pltpu.SemaphoreType.DMA((depth,)),
            pltpu.SemaphoreType.DMA((2,)),
            chip_sem, chip_sem, chip_sem, chip_sem,
            col_sem, col_sem,
            col_sem, col_sem,
            col_sem, col_sem,
            row_sem, row_sem,
            row_sem, row_sem,
            row_sem, row_sem,
        ],
        compiler_params=pltpu.CompilerParams(
            collective_id=0, has_side_effects=True, vmem_limit_bytes=52 * 1024 * 1024
        ),
        cost_estimate=pl.CostEstimate(
            flops=12 * depth * rows * cols * rank,
            bytes_accessed=4 * depth * rows * cols,
            transcendentals=0,
        ),
    )(tensor, factor_b, factor_c)
    anywhere = pl.BlockSpec(memory_space=pl.ANY)
    return pl.pallas_call(
        finish,
        out_shape=shapes,
        in_specs=[anywhere] * 2,
        out_specs=(anywhere, anywhere),
        scratch_shapes=[pltpu.SemaphoreType.DMA((2,))],
        compiler_params=pltpu.CompilerParams(vmem_limit_bytes=1024 * 1024),
    )(*updates)


def solution(mesh):
    placed = (P(None, "row", "col"), P(("col", "row"), None), P())
    return jax.shard_map(
        per_device,
        mesh=mesh,
        in_specs=placed,
        out_specs=(P(("row", "col"), None), P(("col", "row"), None)),
        check_vma=False,
    )
```

```python
import functools

import jax
import jax.numpy as jnp
from jax import lax
from jax.experimental import pallas as pl
from jax.experimental.pallas import tpu as pltpu
from jax.sharding import PartitionSpec as P

EPSILON = 1e-06
MESH = pl.DeviceIdType.MESH
HIGHEST = lax.Precision.HIGHEST
PANEL = 8


def exact_dot(left, right):
    return jnp.dot(left, right, precision=HIGHEST, preferred_element_type=jnp.float32)


def fast_dot(left, right):
    return jnp.dot(left, right, preferred_element_type=jnp.float32)


def split(value):
    high = value.astype(jnp.bfloat16)
    low = (value - high.astype(jnp.float32)).astype(jnp.bfloat16)
    return high, low


def reciprocal(value):
    guess = pl.reciprocal(value, approx=True)
    return guess * (2.0 - value * guess)


def thirds(value):
    high = value.astype(jnp.bfloat16).astype(jnp.float32)
    rest = value - high
    middle = rest.astype(jnp.bfloat16).astype(jnp.float32)
    return high, middle, rest - middle


def outer_product(left, right):
    l0, l1, l2 = thirds(left)
    r0, r1, r2 = thirds(right)
    lefts = jnp.concatenate([l0, l0, l1, l0, l1, l2], axis=0).astype(jnp.bfloat16)
    rights = jnp.concatenate([r0, r1, r0, r2, r1, r0], axis=0).astype(jnp.bfloat16)
    return lax.dot_general(
        lefts, rights, (((0,), (0,)), ((), ())), preferred_element_type=jnp.float32
    )


def negative_inverse(system, beside=None):
    size = system.shape[0]
    groups = size // PANEL
    shape = (PANEL, size)
    lane = lax.broadcasted_iota(jnp.int32, shape, 1)
    sublane = lax.broadcasted_iota(jnp.int32, shape, 0)
    whole_lane = lax.broadcasted_iota(jnp.int32, (groups, PANEL, size), 2)
    diagonal = lax.broadcasted_iota(jnp.int32, (size, size), 0) == lax.broadcasted_iota(
        jnp.int32, (size, size), 1
    )
    squares = jnp.where(diagonal, system, 0.0)
    scales = lax.rsqrt(jnp.sum(squares, axis=0, keepdims=True)) * lax.rsqrt(
        jnp.sum(squares, axis=1, keepdims=True)
    )
    system = (system * scales).reshape(groups, PANEL, size)
    for panel in range(groups):
        base = panel * PANEL
        rows = system[panel]
        inside = (lane >= base) & (lane < base + PANEL)
        target = jnp.where(inside, jnp.where(lane - base == sublane, -1.0, 0.0), rows)
        stack = jnp.stack(
            [jnp.broadcast_to(rows[:, base + t : base + t + 1], shape) for t in range(PANEL)]
            + [target]
        )
        for t in range(0, PANEL, 2):
            first, second, rest = stack[0], stack[1], stack[2:]
            one = jnp.broadcast_to(first[t : t + 1, :], shape)
            both = jnp.broadcast_to(second[t : t + 1, :], shape)
            two = jnp.broadcast_to(second[t + 1 : t + 2, :], shape)
            upper, lower = sublane == t, sublane == t + 1
            scale = reciprocal(one * two - both * both)
            left = jnp.where(upper, -two, jnp.where(lower, both, first * two - second * both))
            right = jnp.where(upper, both, jnp.where(lower, -one, second * one - first * both))
            left, right = left * scale, right * scale
            kept = jnp.where((upper | lower)[None], 0.0, rest)
            stack = kept - (
                left[None] * rest[:, t : t + 1, :] + right[None] * rest[:, t + 1 : t + 2, :]
            )
        own = stack[0]
        if panel + 1 < groups:
            after = system[panel + 1]
            terms = [
                jnp.broadcast_to(after[:, base + t : base + t + 1], shape) * own[t : t + 1, :]
                for t in range(PANEL)
            ]
            while len(terms) > 1:
                terms = [terms[i] + terms[i + 1] for i in range(0, len(terms), 2)]
            ahead = jnp.where(inside, 0.0, after) - terms[0]
        outside = (whole_lane < base) | (whole_lane >= base + PANEL)
        product = outer_product(rows, own).reshape(groups, PANEL, size)
        swept = jnp.where(outside, system, 0.0) - product
        parts = [swept[:panel], own[None]]
        if panel + 1 < groups:
            parts += [ahead[None], swept[panel + 2 :]]
        system = jnp.concatenate([part for part in parts if part.shape[0]], axis=0)
        if beside is not None:
            beside(panel)
    return system.reshape(size, size) * scales


def kernel(
    row_size, col_size,
    tensor, factor_b, factor_c,
    a_out, b_out,
    raw, parts, piece, c_pad, grams, part_a, recv_a, a_all,
    gram_part, gram_recv, gram_all, acc_b, part_b, half_b, sum_b, recv_b,
    load_sem, small_sem, piece_send, piece_recv, pair_send, pair_recv, gramb_send, gramb_recv,
    parta_send, parta_recv, a_send, a_recv,
    gs_send, gs_recv, gg_send, gg_recv, half_sem, partb_send, partb_recv,
):
    depth, rows, cols = raw.shape
    rank = piece.shape[1]
    own_piece = factor_b.shape[0]
    own_a = rows // col_size
    own_b = cols // row_size
    own_g = rank // row_size
    row = lax.axis_index("row")
    col = lax.axis_index("col")

    def row_peer(d):
        return lax.rem(row + d, row_size)

    def col_peer(d):
        return lax.rem(col + d, col_size)

    def block(index, size):
        return pl.ds(pl.multiple_of(index * size, size), size)

    def loads(k):
        return pltpu.make_async_copy(tensor.at[k], raw.at[k], load_sem.at[k])

    piece_load = pltpu.make_async_copy(
        factor_b, piece.at[block(row, own_piece)], small_sem.at[0]
    )
    c_load = pltpu.make_async_copy(factor_c, c_pad.at[pl.ds(0, depth)], small_sem.at[1])
    c_pad[...] = jnp.zeros(c_pad.shape, jnp.float32)
    piece_load.start()
    c_load.start()
    for k in range(depth):
        loads(k).start()

    barrier = pltpu.get_barrier_semaphore()
    for d in range(1, row_size):
        pl.semaphore_signal(barrier, inc=1, device_id=(row_peer(d), col), device_id_type=MESH)
    for d in range(1, col_size):
        pl.semaphore_signal(barrier, inc=1, device_id=(row, col_peer(d)), device_id_type=MESH)
    pl.semaphore_wait(barrier, row_size + col_size - 2)

    def to_row(d, source, target, send, recv):
        return pltpu.make_async_remote_copy(
            src_ref=source, dst_ref=target, send_sem=send.at[d - 1], recv_sem=recv.at[d - 1],
            device_id=(row_peer(d), col), device_id_type=MESH,
        )

    def to_col(d, source, target, send, recv):
        return pltpu.make_async_remote_copy(
            src_ref=source, dst_ref=target, send_sem=send.at[d - 1], recv_sem=recv.at[d - 1],
            device_id=(row, col_peer(d)), device_id_type=MESH,
        )

    pair = row + 1 - 2 * lax.rem(row, 2)
    chips = row_size // 2

    def chip_peer(d):
        return lax.rem(row + 2 * d, row_size)

    def piece_copy(d, owner):
        here = piece.at[block(owner, own_piece)]
        return pltpu.make_async_remote_copy(
            src_ref=here, dst_ref=here, send_sem=piece_send.at[d], recv_sem=piece_recv.at[d],
            device_id=(chip_peer(d), col), device_id_type=MESH,
        )

    def pair_copy(d, owner):
        here = piece.at[block(owner, own_piece)]
        return pltpu.make_async_remote_copy(
            src_ref=here, dst_ref=here, send_sem=pair_send.at[d], recv_sem=pair_recv.at[d],
            device_id=(pair, col), device_id_type=MESH,
        )

    def partners(d):
        owner = chip_peer(chips - d)
        return owner + 1 - 2 * lax.rem(owner, 2)

    piece_load.wait()
    for d in range(1, chips):
        piece_copy(d, row).start()
    pair_copy(0, row).start()

    step = 64
    for k in range(depth):
        loads(k).wait()

        def split_rows(index, carry):
            here = block(index, step)
            parts[k, here, :cols], parts[k, here, cols:] = split(raw[k, here, :])
            return carry

        lax.fori_loop(0, rows // step, split_rows, 0)

    for d in range(1, chips):
        owner = chip_peer(chips - d)
        piece_copy(d, owner).wait_recv()
        pair_copy(d, owner).start()

    c_load.wait()
    c_rows = c_pad[...]
    c_cols = c_rows.T
    c_gram = c_cols[:, 0:1] * c_rows[0:1, :]
    for k in range(1, depth):
        c_gram = c_gram + c_cols[:, k : k + 1] * c_rows[k : k + 1, :]

    pair_copy(0, pair).wait_recv()
    for d in range(1, chips):
        pair_copy(d, partners(d)).wait_recv()

    whole = piece[...]
    grams[col] = exact_dot(whole.T, whole)

    def gramb_copy(d, owner):
        return to_col(d, grams.at[owner], grams.at[owner], gramb_send, gramb_recv)

    for d in range(1, col_size):
        gramb_copy(d, col).start()

    piece_high, piece_low = split(whole)
    both = jnp.concatenate(
        [
            jnp.concatenate([piece_high, piece_low], axis=1),
            jnp.concatenate([piece_high, jnp.zeros_like(piece_low)], axis=1),
        ],
        axis=0,
    )

    def parta_copy(d, slot):
        return to_col(
            d, part_a.at[block(col_peer(d), own_a)], recv_a.at[slot], parta_send, parta_recv
        )

    group = 4 if depth % 4 == 0 else 1
    for d in list(range(1, col_size)) + [0]:
        owner = col_peer(d)
        here = block(owner, own_a)
        if d == 0:
            for other in range(1, col_size):
                gramb_copy(other, col_peer(col_size - other)).wait_recv()
            gram_b = grams[0]
            for index in range(1, col_size):
                gram_b = gram_b + grams[index]
        total = jnp.zeros((own_a, rank), jnp.float32)
        for first in range(0, depth, group):
            span = slice(first, first + group)
            product = fast_dot(parts[span, here, :].reshape(group * own_a, 2 * cols), both)
            summed = product[:, :rank] + product[:, rank:]
            for k in range(group):
                total = total + summed[k * own_a : (k + 1) * own_a] * c_rows[first + k : first + k + 1, :]
        if d:
            part_a[here, :] = total
            parta_copy(d, d - 1).start()
        else:
            mine = total

    solve_a = negative_inverse(c_gram * gram_b)

    for d in range(1, col_size):
        parta_copy(d, d - 1).wait_recv()
        mine = mine + recv_a[d - 1]
    a_update = -exact_dot(mine, solve_a)
    a_out[...] = a_update
    a_all[block(col, own_a), :] = a_update

    def a_copy(d, owner):
        here = a_all.at[block(owner, own_a)]
        return to_col(d, here, here, a_send, a_recv)

    for d in range(1, col_size):
        a_copy(d, col).start()
    for d in range(1, col_size):
        a_copy(d, col_peer(col_size - d)).wait_recv()

    factor = a_all[...]
    turned = factor.T
    gram_part[...] = exact_dot(turned, factor)

    def gs_copy(d, slot):
        return to_row(
            d, gram_part.at[block(row_peer(d), own_g)], gram_recv.at[slot], gs_send, gs_recv
        )

    for d in range(1, row_size):
        gs_copy(d, d - 1).start()

    turned_high, turned_low = split(turned)
    stacked = jnp.concatenate([turned_high, turned_low], axis=0)

    def mode_two(k):
        left = fast_dot(stacked, parts[k, :, :cols])
        right = fast_dot(turned_high, parts[k, :, cols:])
        term = (left[:rank] + (left[rank:] + right)) * c_cols[:, k : k + 1]
        if k:
            acc_b[...] += term
        else:
            acc_b[...] = term

    half = depth // 2
    for k in range(half):
        mode_two(k)

    for d in range(1, row_size):
        gs_copy(d, d - 1).wait_recv()
    owned = gram_part[block(row, own_g), :]
    for d in range(1, row_size):
        owned = owned + gram_recv[d - 1]
    gram_all[block(row, own_g), :] = owned

    def gg_copy(d, owner):
        here = gram_all.at[block(owner, own_g)]
        return to_row(d, here, here, gg_send, gg_recv)

    for d in range(1, row_size):
        gg_copy(d, row).start()

    for k in range(half, depth):
        mode_two(k)
    core = lax.rem(row, 2)
    chip = lax.div(row, 2)
    turned_b = acc_b[...].T
    for owner in range(row_size):
        spot = slice(owner // 2 * own_b, (owner // 2 + 1) * own_b)
        part_b[owner % 2, spot, :] = turned_b[owner * own_b : (owner + 1) * own_b]

    half_copy = pltpu.make_async_remote_copy(
        src_ref=part_b.at[1 - core], dst_ref=half_b, send_sem=half_sem.at[0],
        recv_sem=half_sem.at[1], device_id=(pair, col), device_id_type=MESH,
    )
    half_copy.start()

    def partb_copy(d):
        return pltpu.make_async_remote_copy(
            src_ref=sum_b.at[block(lax.rem(chip + d, chips), own_b)], dst_ref=recv_b.at[d - 1],
            send_sem=partb_send.at[d], recv_sem=partb_recv.at[d],
            device_id=(chip_peer(d), col), device_id_type=MESH,
        )

    def beside_b(panel):
        if panel == 3:
            half_copy.wait_recv()
            sum_b[...] = part_b[core] + half_b[...]
            for d in range(1, chips):
                partb_copy(d).start()

    for d in range(1, row_size):
        gg_copy(d, row_peer(row_size - d)).wait_recv()
    gram_a = gram_all[...]
    diagonal = lax.broadcasted_iota(jnp.int32, (rank, rank), 0) == lax.broadcasted_iota(
        jnp.int32, (rank, rank), 1
    )
    squares = jnp.where(diagonal, gram_a, 0.0)
    inv_row = 1.0 / jnp.sqrt(jnp.sum(squares, axis=0, keepdims=True) + EPSILON)
    inv_col = 1.0 / jnp.sqrt(jnp.sum(squares, axis=1, keepdims=True) + EPSILON)
    solve_b = negative_inverse(c_gram * (gram_a * inv_row * inv_col), beside_b)

    mine = sum_b[block(chip, own_b), :]
    for d in range(1, chips):
        partb_copy(d).wait_recv()
        mine = mine + recv_b[d - 1]
    b_out[...] = -exact_dot(mine * inv_row, solve_b)

    half_copy.wait_send()
    pair_copy(0, row).wait_send()
    for d in range(1, chips):
        partb_copy(d).wait_send()
        piece_copy(d, row).wait_send()
        pair_copy(d, chip_peer(chips - d)).wait_send()
    for d in range(1, row_size):
        gs_copy(d, d - 1).wait_send()
        gg_copy(d, row).wait_send()
    for d in range(1, col_size):
        gramb_copy(d, col).wait_send()
        parta_copy(d, d - 1).wait_send()
        a_copy(d, col).wait_send()


def finish(a_update, b_update, a_out, b_out, sems):
    copies = [
        pltpu.make_async_copy(a_update, a_out, sems.at[0]),
        pltpu.make_async_copy(b_update, b_out, sems.at[1]),
    ]
    for copy in copies:
        copy.start()
    for copy in copies:
        copy.wait()


def per_device(tensor, factor_b, factor_c):
    depth, rows, cols = tensor.shape
    rank = factor_c.shape[1]
    row_size, col_size = lax.axis_size("row"), lax.axis_size("col")
    own_a, own_b, own_g = rows // col_size, cols // row_size, rank // row_size
    f32, bf16 = jnp.float32, jnp.bfloat16
    vmem = pltpu.VMEM
    row_sem = pltpu.SemaphoreType.DMA((row_size - 1,))
    col_sem = pltpu.SemaphoreType.DMA((col_size - 1,))
    chip_sem = pltpu.SemaphoreType.DMA((row_size // 2,))
    in_vmem = pl.BlockSpec(memory_space=pltpu.VMEM)
    shapes = (
        jax.ShapeDtypeStruct((own_a, rank), f32),
        jax.ShapeDtypeStruct((own_b, rank), f32),
    )
    updates = pl.pallas_call(
        functools.partial(kernel, row_size, col_size),
        out_shape=shapes,
        in_specs=[pl.BlockSpec(memory_space=pltpu.HBM)] * 3,
        out_specs=(in_vmem, in_vmem),
        scratch_shapes=[
            vmem((depth, rows, cols), f32),
            vmem((depth, rows, 2 * cols), bf16),
            vmem((cols, rank), f32),
            vmem((rank, rank), f32),
            vmem((col_size, rank, rank), f32),
            vmem((rows, rank), f32),
            vmem((col_size - 1, own_a, rank), f32),
            vmem((rows, rank), f32),
            vmem((rank, rank), f32),
            vmem((row_size - 1, own_g, rank), f32),
            vmem((rank, rank), f32),
            vmem((rank, cols), f32),
            vmem((2, cols // 2, rank), f32),
            vmem((cols // 2, rank), f32),
            vmem((cols // 2, rank), f32),
            vmem((row_size // 2, own_b, rank), f32),
            pltpu.SemaphoreType.DMA((depth,)),
            pltpu.SemaphoreType.DMA((2,)),
            chip_sem, chip_sem, chip_sem, chip_sem,
            col_sem, col_sem,
            col_sem, col_sem,
            col_sem, col_sem,
            row_sem, row_sem,
            row_sem, row_sem,
            pltpu.SemaphoreType.DMA((2,)),
            chip_sem, chip_sem,
        ],
        compiler_params=pltpu.CompilerParams(
            collective_id=0, has_side_effects=True, vmem_limit_bytes=52 * 1024 * 1024
        ),
        cost_estimate=pl.CostEstimate(
            flops=12 * depth * rows * cols * rank,
            bytes_accessed=4 * depth * rows * cols,
            transcendentals=0,
        ),
    )(tensor, factor_b, factor_c)
    anywhere = pl.BlockSpec(memory_space=pl.ANY)
    return pl.pallas_call(
        finish,
        out_shape=shapes,
        in_specs=[anywhere] * 2,
        out_specs=(anywhere, anywhere),
        scratch_shapes=[pltpu.SemaphoreType.DMA((2,))],
        compiler_params=pltpu.CompilerParams(vmem_limit_bytes=1024 * 1024),
    )(*updates)


def solution(mesh):
    placed = (P(None, "row", "col"), P(("col", "row"), None), P())
    return jax.shard_map(
        per_device,
        mesh=mesh,
        in_specs=placed,
        out_specs=(P(("row", "col"), None), P(("col", "row"), None)),
        check_vma=False,
    )
```

```python
import functools

import jax
import jax.numpy as jnp
from jax import lax
from jax.experimental import pallas as pl
from jax.experimental.pallas import tpu as pltpu
from jax.sharding import PartitionSpec as P

EPSILON = 1e-06
MESH = pl.DeviceIdType.MESH
HIGHEST = lax.Precision.HIGHEST
PANEL = 8


def exact_dot(left, right):
    return jnp.dot(left, right, precision=HIGHEST, preferred_element_type=jnp.float32)


def fast_dot(left, right):
    return jnp.dot(left, right, preferred_element_type=jnp.float32)


def split(value):
    high = value.astype(jnp.bfloat16)
    low = (value - high.astype(jnp.float32)).astype(jnp.bfloat16)
    return high, low


def reciprocal(value):
    guess = pl.reciprocal(value, approx=True)
    return guess * (2.0 - value * guess)


def thirds(value):
    high = value.astype(jnp.bfloat16).astype(jnp.float32)
    rest = value - high
    middle = rest.astype(jnp.bfloat16).astype(jnp.float32)
    return high, middle, rest - middle


def outer_product(left, right):
    l0, l1, l2 = thirds(left)
    r0, r1, r2 = thirds(right)
    lefts = jnp.concatenate([l0, l0, l1, l0, l1, l2], axis=0).astype(jnp.bfloat16)
    rights = jnp.concatenate([r0, r1, r0, r2, r1, r0], axis=0).astype(jnp.bfloat16)
    return lax.dot_general(
        lefts, rights, (((0,), (0,)), ((), ())), preferred_element_type=jnp.float32
    )


def negative_inverse(system):
    size = system.shape[0]
    groups = size // PANEL
    shape = (PANEL, size)
    lane = lax.broadcasted_iota(jnp.int32, shape, 1)
    sublane = lax.broadcasted_iota(jnp.int32, shape, 0)
    whole_lane = lax.broadcasted_iota(jnp.int32, (groups, PANEL, size), 2)
    diagonal = lax.broadcasted_iota(jnp.int32, (size, size), 0) == lax.broadcasted_iota(
        jnp.int32, (size, size), 1
    )
    squares = jnp.where(diagonal, system, 0.0)
    scales = lax.rsqrt(jnp.sum(squares, axis=0, keepdims=True)) * lax.rsqrt(
        jnp.sum(squares, axis=1, keepdims=True)
    )
    system = (system * scales).reshape(groups, PANEL, size)
    for panel in range(groups):
        base = panel * PANEL
        rows = system[panel]
        inside = (lane >= base) & (lane < base + PANEL)
        target = jnp.where(inside, jnp.where(lane - base == sublane, -1.0, 0.0), rows)
        stack = jnp.stack(
            [jnp.broadcast_to(rows[:, base + t : base + t + 1], shape) for t in range(PANEL)]
            + [target]
        )
        for t in range(0, PANEL, 2):
            first, second, rest = stack[0], stack[1], stack[2:]
            one = jnp.broadcast_to(first[t : t + 1, :], shape)
            both = jnp.broadcast_to(second[t : t + 1, :], shape)
            two = jnp.broadcast_to(second[t + 1 : t + 2, :], shape)
            upper, lower = sublane == t, sublane == t + 1
            scale = reciprocal(one * two - both * both)
            left = jnp.where(upper, -two, jnp.where(lower, both, first * two - second * both))
            right = jnp.where(upper, both, jnp.where(lower, -one, second * one - first * both))
            left, right = left * scale, right * scale
            kept = jnp.where((upper | lower)[None], 0.0, rest)
            stack = kept - (
                left[None] * rest[:, t : t + 1, :] + right[None] * rest[:, t + 1 : t + 2, :]
            )
        own = stack[0]
        if panel + 1 < groups:
            after = system[panel + 1]
            terms = [
                jnp.broadcast_to(after[:, base + t : base + t + 1], shape) * own[t : t + 1, :]
                for t in range(PANEL)
            ]
            while len(terms) > 1:
                terms = [terms[i] + terms[i + 1] for i in range(0, len(terms), 2)]
            ahead = jnp.where(inside, 0.0, after) - terms[0]
        outside = (whole_lane < base) | (whole_lane >= base + PANEL)
        product = outer_product(rows, own).reshape(groups, PANEL, size)
        swept = jnp.where(outside, system, 0.0) - product
        parts = [swept[:panel], own[None]]
        if panel + 1 < groups:
            parts += [ahead[None], swept[panel + 2 :]]
        system = jnp.concatenate([part for part in parts if part.shape[0]], axis=0)
    return system.reshape(size, size) * scales


def kernel(
    row_size, col_size,
    tensor, factor_b, factor_c,
    a_out, b_out,
    raw, parts, piece, c_pad, grams, part_a, recv_a, a_all,
    gram_part, gram_recv, gram_all, acc_b, part_b, recv_b,
    load_sem, small_sem, piece_send, piece_recv, pair_send, pair_recv, gramb_send, gramb_recv,
    parta_send, parta_recv, a_send, a_recv,
    gs_send, gs_recv, gg_send, gg_recv, partb_send, partb_recv,
):
    depth, rows, cols = raw.shape
    rank = piece.shape[1]
    own_piece = factor_b.shape[0]
    own_a = rows // col_size
    own_b = cols // row_size
    own_g = rank // row_size
    row = lax.axis_index("row")
    col = lax.axis_index("col")

    def row_peer(d):
        return lax.rem(row + d, row_size)

    def col_peer(d):
        return lax.rem(col + d, col_size)

    def block(index, size):
        return pl.ds(pl.multiple_of(index * size, size), size)

    def loads(k):
        return pltpu.make_async_copy(tensor.at[k], raw.at[k], load_sem.at[k])

    piece_load = pltpu.make_async_copy(
        factor_b, piece.at[block(row, own_piece)], small_sem.at[0]
    )
    c_load = pltpu.make_async_copy(factor_c, c_pad.at[pl.ds(0, depth)], small_sem.at[1])
    c_pad[...] = jnp.zeros(c_pad.shape, jnp.float32)
    piece_load.start()
    c_load.start()
    for k in range(depth):
        loads(k).start()

    barrier = pltpu.get_barrier_semaphore()
    for d in range(1, row_size):
        pl.semaphore_signal(barrier, inc=1, device_id=(row_peer(d), col), device_id_type=MESH)
    for d in range(1, col_size):
        pl.semaphore_signal(barrier, inc=1, device_id=(row, col_peer(d)), device_id_type=MESH)
    pl.semaphore_wait(barrier, row_size + col_size - 2)

    def to_row(d, source, target, send, recv):
        return pltpu.make_async_remote_copy(
            src_ref=source, dst_ref=target, send_sem=send.at[d - 1], recv_sem=recv.at[d - 1],
            device_id=(row_peer(d), col), device_id_type=MESH,
        )

    def to_col(d, source, target, send, recv):
        return pltpu.make_async_remote_copy(
            src_ref=source, dst_ref=target, send_sem=send.at[d - 1], recv_sem=recv.at[d - 1],
            device_id=(row, col_peer(d)), device_id_type=MESH,
        )

    pair = row + 1 - 2 * lax.rem(row, 2)
    chips = row_size // 2

    def chip_peer(d):
        return lax.rem(row + 2 * d, row_size)

    def piece_copy(d, owner):
        here = piece.at[block(owner, own_piece)]
        return pltpu.make_async_remote_copy(
            src_ref=here, dst_ref=here, send_sem=piece_send.at[d], recv_sem=piece_recv.at[d],
            device_id=(chip_peer(d), col), device_id_type=MESH,
        )

    def pair_copy(d, owner):
        here = piece.at[block(owner, own_piece)]
        return pltpu.make_async_remote_copy(
            src_ref=here, dst_ref=here, send_sem=pair_send.at[d], recv_sem=pair_recv.at[d],
            device_id=(pair, col), device_id_type=MESH,
        )

    def partners(d):
        owner = chip_peer(chips - d)
        return owner + 1 - 2 * lax.rem(owner, 2)

    piece_load.wait()
    for d in range(1, chips):
        piece_copy(d, row).start()
    pair_copy(0, row).start()

    step = 64
    for k in range(depth):
        loads(k).wait()

        def split_rows(index, carry):
            here = block(index, step)
            parts[k, here, :cols], parts[k, here, cols:] = split(raw[k, here, :])
            return carry

        lax.fori_loop(0, rows // step, split_rows, 0)

    for d in range(1, chips):
        owner = chip_peer(chips - d)
        piece_copy(d, owner).wait_recv()
        pair_copy(d, owner).start()

    c_load.wait()
    c_rows = c_pad[...]
    c_cols = c_rows.T
    c_gram = c_cols[:, 0:1] * c_rows[0:1, :]
    for k in range(1, depth):
        c_gram = c_gram + c_cols[:, k : k + 1] * c_rows[k : k + 1, :]

    pair_copy(0, pair).wait_recv()
    for d in range(1, chips):
        pair_copy(d, partners(d)).wait_recv()

    whole = piece[...]
    grams[col] = exact_dot(whole.T, whole)

    def gramb_copy(d, owner):
        return to_col(d, grams.at[owner], grams.at[owner], gramb_send, gramb_recv)

    for d in range(1, col_size):
        gramb_copy(d, col).start()

    piece_high, piece_low = split(whole)
    both = jnp.concatenate(
        [
            jnp.concatenate([piece_high, piece_low], axis=1),
            jnp.concatenate([piece_high, jnp.zeros_like(piece_low)], axis=1),
        ],
        axis=0,
    )

    def parta_copy(d, slot):
        return to_col(
            d, part_a.at[block(col_peer(d), own_a)], recv_a.at[slot], parta_send, parta_recv
        )

    group = 4 if depth % 4 == 0 else 1
    for d in list(range(1, col_size)) + [0]:
        owner = col_peer(d)
        here = block(owner, own_a)
        total = jnp.zeros((own_a, rank), jnp.float32)
        for first in range(0, depth, group):
            span = slice(first, first + group)
            product = fast_dot(parts[span, here, :].reshape(group * own_a, 2 * cols), both)
            summed = product[:, :rank] + product[:, rank:]
            for k in range(group):
                total = total + summed[k * own_a : (k + 1) * own_a] * c_rows[first + k : first + k + 1, :]
        if d:
            part_a[here, :] = total
            parta_copy(d, d - 1).start()
        else:
            mine = total

    for d in range(1, col_size):
        gramb_copy(d, col_peer(col_size - d)).wait_recv()
    gram_b = grams[0]
    for index in range(1, col_size):
        gram_b = gram_b + grams[index]
    solve_a = negative_inverse(c_gram * gram_b)

    for d in range(1, col_size):
        parta_copy(d, d - 1).wait_recv()
        mine = mine + recv_a[d - 1]
    a_update = -exact_dot(mine, solve_a)
    a_out[...] = a_update
    a_all[block(col, own_a), :] = a_update

    def a_copy(d, owner):
        here = a_all.at[block(owner, own_a)]
        return to_col(d, here, here, a_send, a_recv)

    for d in range(1, col_size):
        a_copy(d, col).start()
    for d in range(1, col_size):
        a_copy(d, col_peer(col_size - d)).wait_recv()

    factor = a_all[...]
    turned = factor.T
    gram_part[...] = exact_dot(turned, factor)

    def gs_copy(d, slot):
        return to_row(
            d, gram_part.at[block(row_peer(d), own_g)], gram_recv.at[slot], gs_send, gs_recv
        )

    for d in range(1, row_size):
        gs_copy(d, d - 1).start()

    turned_high, turned_low = split(turned)
    stacked = jnp.concatenate([turned_high, turned_low], axis=0)

    def mode_two(k):
        left = fast_dot(stacked, parts[k, :, :cols])
        right = fast_dot(turned_high, parts[k, :, cols:])
        term = (left[:rank] + (left[rank:] + right)) * c_cols[:, k : k + 1]
        if k:
            acc_b[...] += term
        else:
            acc_b[...] = term

    half = depth // 2
    for k in range(half):
        mode_two(k)

    for d in range(1, row_size):
        gs_copy(d, d - 1).wait_recv()
    owned = gram_part[block(row, own_g), :]
    for d in range(1, row_size):
        owned = owned + gram_recv[d - 1]
    gram_all[block(row, own_g), :] = owned

    def gg_copy(d, owner):
        here = gram_all.at[block(owner, own_g)]
        return to_row(d, here, here, gg_send, gg_recv)

    for d in range(1, row_size):
        gg_copy(d, row).start()

    for k in range(half, depth):
        mode_two(k)
    part_b[...] = acc_b[...].T

    def partb_copy(d, slot):
        return to_row(
            d, part_b.at[block(row_peer(d), own_b)], recv_b.at[slot], partb_send, partb_recv
        )

    for d in range(1, row_size):
        partb_copy(d, d - 1).start()

    for d in range(1, row_size):
        gg_copy(d, row_peer(row_size - d)).wait_recv()
    gram_a = gram_all[...]
    diagonal = lax.broadcasted_iota(jnp.int32, (rank, rank), 0) == lax.broadcasted_iota(
        jnp.int32, (rank, rank), 1
    )
    squares = jnp.where(diagonal, gram_a, 0.0)
    inv_row = 1.0 / jnp.sqrt(jnp.sum(squares, axis=0, keepdims=True) + EPSILON)
    inv_col = 1.0 / jnp.sqrt(jnp.sum(squares, axis=1, keepdims=True) + EPSILON)
    solve_b = negative_inverse(c_gram * (gram_a * inv_row * inv_col))

    mine = part_b[block(row, own_b), :]
    for d in range(1, row_size):
        partb_copy(d, d - 1).wait_recv()
        mine = mine + recv_b[d - 1]
    b_out[...] = -exact_dot(mine * inv_row, solve_b)

    pair_copy(0, row).wait_send()
    for d in range(1, chips):
        piece_copy(d, row).wait_send()
        pair_copy(d, chip_peer(chips - d)).wait_send()
    for d in range(1, row_size):
        gs_copy(d, d - 1).wait_send()
        gg_copy(d, row).wait_send()
        partb_copy(d, d - 1).wait_send()
    for d in range(1, col_size):
        gramb_copy(d, col).wait_send()
        parta_copy(d, d - 1).wait_send()
        a_copy(d, col).wait_send()


def finish(a_update, b_update, a_out, b_out, sems):
    copies = [
        pltpu.make_async_copy(a_update, a_out, sems.at[0]),
        pltpu.make_async_copy(b_update, b_out, sems.at[1]),
    ]
    for copy in copies:
        copy.start()
    for copy in copies:
        copy.wait()


def per_device(tensor, factor_b, factor_c):
    depth, rows, cols = tensor.shape
    rank = factor_c.shape[1]
    row_size, col_size = lax.axis_size("row"), lax.axis_size("col")
    own_a, own_b, own_g = rows // col_size, cols // row_size, rank // row_size
    f32, bf16 = jnp.float32, jnp.bfloat16
    vmem = pltpu.VMEM
    row_sem = pltpu.SemaphoreType.DMA((row_size - 1,))
    col_sem = pltpu.SemaphoreType.DMA((col_size - 1,))
    chip_sem = pltpu.SemaphoreType.DMA((row_size // 2,))
    in_vmem = pl.BlockSpec(memory_space=pltpu.VMEM)
    shapes = (
        jax.ShapeDtypeStruct((own_a, rank), f32),
        jax.ShapeDtypeStruct((own_b, rank), f32),
    )
    updates = pl.pallas_call(
        functools.partial(kernel, row_size, col_size),
        out_shape=shapes,
        in_specs=[pl.BlockSpec(memory_space=pltpu.HBM)] * 3,
        out_specs=(in_vmem, in_vmem),
        scratch_shapes=[
            vmem((depth, rows, cols), f32),
            vmem((depth, rows, 2 * cols), bf16),
            vmem((cols, rank), f32),
            vmem((rank, rank), f32),
            vmem((col_size, rank, rank), f32),
            vmem((rows, rank), f32),
            vmem((col_size - 1, own_a, rank), f32),
            vmem((rows, rank), f32),
            vmem((rank, rank), f32),
            vmem((row_size - 1, own_g, rank), f32),
            vmem((rank, rank), f32),
            vmem((rank, cols), f32),
            vmem((cols, rank), f32),
            vmem((row_size - 1, own_b, rank), f32),
            pltpu.SemaphoreType.DMA((depth,)),
            pltpu.SemaphoreType.DMA((2,)),
            chip_sem, chip_sem, chip_sem, chip_sem,
            col_sem, col_sem,
            col_sem, col_sem,
            col_sem, col_sem,
            row_sem, row_sem,
            row_sem, row_sem,
            row_sem, row_sem,
        ],
        compiler_params=pltpu.CompilerParams(
            collective_id=0, has_side_effects=True, vmem_limit_bytes=52 * 1024 * 1024
        ),
        cost_estimate=pl.CostEstimate(
            flops=12 * depth * rows * cols * rank,
            bytes_accessed=4 * depth * rows * cols,
            transcendentals=0,
        ),
    )(tensor, factor_b, factor_c)
    anywhere = pl.BlockSpec(memory_space=pl.ANY)
    return pl.pallas_call(
        finish,
        out_shape=shapes,
        in_specs=[anywhere] * 2,
        out_specs=(anywhere, anywhere),
        scratch_shapes=[pltpu.SemaphoreType.DMA((2,))],
        compiler_params=pltpu.CompilerParams(vmem_limit_bytes=1024 * 1024),
    )(*updates)


def solution(mesh):
    placed = (P(None, "row", "col"), P(("col", "row"), None), P())
    return jax.shard_map(
        per_device,
        mesh=mesh,
        in_specs=placed,
        out_specs=(P(("row", "col"), None), P(("col", "row"), None)),
        check_vma=False,
    )
```
